512 devices in a mesh: ctx: 64 (over x, y_lo, z), tp: 8 (over y_hi, core).
Axes of the slice: x: 4, y: 8 (y_hi: 4, y_lo: 2; y = y_hi * 2 + y_lo), z: 8, core: 2. Of those that a mesh axis runs over, the one named last changes fastest.
Arguments:
- features: bfloat16 [8192, 4096], P('ctx'), may hold values from -6 to 6
- grad_out: bfloat16 [8192, 4096], P('ctx'), may hold values from -6 to 6
- w_value: bfloat16 [4096, 4096], P('ctx', 'tp'), may hold values from -0.09375 to 0.09375
- w_query: bfloat16 [4096, 4096], P('ctx', 'tp'), may hold values from -0.09375 to 0.09375
- w_out: bfloat16 [4096, 4096], P('tp', 'ctx'), may hold values from -0.09375 to 0.09375
- residues: float32 [16, 4096], P(None, 'tp'), may hold values from -0.3 to 0.3
- decays: float32 [16, 4096], P(None, 'tp'), may hold values from 3.0517578e-05 to 0.05
- freqs: float32 [16, 4096], P(None, 'tp'), may hold values from 0 to 0.2
- skips: float32 [4096], P('tp'), may hold values from 0.5 to 1.5
Outputs:
- mixed: bfloat16 [8192, 4096], P('ctx', 'tp')
- grad_in: bfloat16 [8192, 4096], P('ctx', 'tp')
- grad_residues: float32 [16, 4096], P(None, ('tp', 'ctx'))
The draws below stay inside these ranges and needn't reach their ends.
All inputs are finite; a program needn't handle non-finite values.
Results may differ from the reference program's by a relative error of at most 0.023.
Values may be sent and summed in bfloat16 or wider, within the bound.
A program may use at most 128 MiB of HBM per device.

```python
import math
import jax
import jax.numpy as jnp
from jax import lax

D = 4096
CH = 4096
ORDER = 16
SEQ = 8192
CH_DEV = 512
N_TP = 8


def block_scale(key, dims, split, least, high):
    factor_of, own = 1.0, jax.random.fold_in(key, 6)
    for axis_at, parts in split:
        draws = jnp.exp(jax.random.uniform(jax.random.fold_in(own, axis_at), (parts,), jnp.float32, least / len(split), high / len(split)))
        factor_of = factor_of * jnp.repeat(draws, dims[axis_at] // parts).reshape([-1 if axis == axis_at else 1 for axis in range(len(dims))])
    return factor_of


def noise(rng, dims, deviation, most, cuts=(), dtype=jnp.bfloat16):
    level = block_scale(rng, dims, cuts, -0.22, 0.18) if cuts else 1.0
    values = jax.random.normal(rng, dims, jnp.float32) * deviation * level
    return jnp.minimum(jnp.maximum(values, -most), most).astype(dtype)


def setup_inputs(seed: int = 0) -> dict:
    splits = jax.random.split(jax.random.key(seed), 10)
    features = noise(splits[0], (SEQ, D), 1.0, 6.0, ((0, 64),))
    grad_out = noise(splits[1], (SEQ, D), 1.0, 6.0, ((0, 64),))
    w_value = noise(splits[2], (D, CH), D ** -0.5, 0.09375, ((0, 64), (1, 8)))
    w_query = noise(splits[3], (D, CH), D ** -0.5, 0.09375, ((0, 64), (1, 8)))
    w_out = noise(splits[4], (CH, D), CH ** -0.5, 0.09375, ((0, 8), (1, 64)))
    residues = noise(splits[5], (ORDER, CH), 0.05, 0.3, ((1, 8),), jnp.float32)
    decays = jnp.clip(jnp.exp(math.log(0.05) - 7.4014754 * jax.random.uniform(splits[6], (ORDER, CH), jnp.float32) ** block_scale(splits[6], (ORDER, CH), ((1, 8),), -0.2, 0.2)), 3.0517578125e-05, 0.05)
    freqs = jnp.clip(0.2 * jax.random.uniform(splits[7], (ORDER, CH), jnp.float32) ** block_scale(splits[7], (ORDER, CH), ((1, 8),), -0.2, 0.2), 0.0, 0.2)
    skips = jnp.clip(0.5 + 1.0 * jax.random.uniform(splits[8], (CH,), jnp.float32) ** block_scale(splits[8], (CH,), ((0, 8),), -0.2, 0.2), 0.5, 1.5)
    return {"features": features, "grad_out": grad_out, "w_value": w_value, "w_query": w_query, "w_out": w_out, "residues": residues, "decays": decays, "freqs": freqs, "skips": skips}


def mode_basis(decay_row, freq_row, positions):
    return jnp.exp(-decay_row[None, :] * positions[:, None]) * jnp.cos(freq_row[None, :] * positions[:, None])


def group_terms(group, value, query, features, grad_out, w_value, w_query, w_out, residues, decays, freqs, skips):
    start = group * CH_DEV
    cols = lambda arr: lax.dynamic_slice_in_dim(arr, start, CH_DEV, arr.ndim - 1)
    value_grp = cols(value).astype(jnp.float32)
    query_grp = cols(query).astype(jnp.float32)
    res_grp = cols(residues)
    dec_grp = cols(decays)
    fre_grp = cols(freqs)
    skip_grp = cols(skips)
    positions = jnp.arange(SEQ).astype(jnp.float32)
    filt = jnp.zeros((SEQ, CH_DEV), jnp.float32)
    for mode in range(ORDER):
        filt = filt + res_grp[mode][None, :] * mode_basis(dec_grp[mode], fre_grp[mode], positions)
    total = 2 * SEQ
    value_spec = jnp.fft.rfft(value_grp, total, axis=0)
    filt_spec = jnp.fft.rfft(filt, total, axis=0)
    conv = jnp.fft.irfft(value_spec * filt_spec, total, axis=0)[:SEQ]
    state = (conv + skip_grp[None, :] * value_grp).astype(jnp.bfloat16)
    gated = (query_grp * state.astype(jnp.float32)).astype(jnp.bfloat16)
    out_rows = lax.dynamic_slice_in_dim(w_out, start, CH_DEV, 0)
    mixed_part = jnp.dot(gated, out_rows, preferred_element_type=jnp.float32).astype(jnp.bfloat16)
    mixed_part = lax.optimization_barrier(mixed_part).astype(jnp.float32)
    grad_gated = jnp.dot(grad_out, out_rows.T, preferred_element_type=jnp.float32)
    grad_query = (grad_gated * state.astype(jnp.float32)).astype(jnp.bfloat16)
    grad_state = (grad_gated * query_grp).astype(jnp.bfloat16)
    grad_state_f = grad_state.astype(jnp.float32)
    grad_spec = jnp.fft.rfft(grad_state_f, total, axis=0)
    back = jnp.fft.irfft(grad_spec * jnp.conj(filt_spec), total, axis=0)[:SEQ]
    grad_value = (back + skip_grp[None, :] * grad_state_f).astype(jnp.bfloat16)
    grad_filt = jnp.fft.irfft(grad_spec * jnp.conj(value_spec), total, axis=0)[:SEQ]
    grad_res = []
    for mode in range(ORDER):
        grad_res.append(jnp.sum(grad_filt * mode_basis(dec_grp[mode], fre_grp[mode], positions), axis=0))
    grad_res = jnp.stack(grad_res, axis=0)
    wq_grp = cols(w_query)
    wv_grp = cols(w_value)
    grad_part = jnp.dot(grad_query, wq_grp.T, preferred_element_type=jnp.float32) + jnp.dot(grad_value, wv_grp.T, preferred_element_type=jnp.float32)
    grad_part = lax.optimization_barrier(grad_part.astype(jnp.bfloat16)).astype(jnp.float32)
    return mixed_part, grad_part, grad_res


def reference(features, grad_out, w_value, w_query, w_out, residues, decays, freqs, skips):
    value = jnp.dot(features, w_value, preferred_element_type=jnp.float32).astype(jnp.bfloat16)
    query = jnp.dot(features, w_query, preferred_element_type=jnp.float32).astype(jnp.bfloat16)

    def one_group(group):
        return group_terms(group, value, query, features, grad_out, w_value, w_query, w_out, residues, decays, freqs, skips)

    mixed_parts, grad_parts, grad_res = lax.map(one_group, jnp.arange(N_TP).astype(jnp.int32))
    mixed = jnp.sum(mixed_parts, axis=0).astype(jnp.bfloat16)
    grad_in = jnp.sum(grad_parts, axis=0).astype(jnp.bfloat16)
    grad_residues = jnp.transpose(grad_res, (1, 0, 2)).reshape(ORDER, CH)
    return mixed, grad_in, grad_residues
```

```python
import functools

import jax
import jax.numpy as jnp
from jax import lax
from jax.experimental import pallas as pl
from jax.experimental.pallas import tpu as pltpu
from jax.sharding import PartitionSpec as P

MESH = pl.DeviceIdType.MESH
F32, BF16 = jnp.float32, jnp.bfloat16
NX, NY, NZ = 4, 2, 8
NCTX, NTP = 64, 8
ROWS = 64
HALF = ROWS // 2
CG = 512
TOK = 128
CB = 8
ORDER = 16
LANES = CB * ORDER
NK = 13

NN = (((1,), (0,)), ((), ()))
NT = (((1,), (1,)), ((), ()))


def dot(a, b, dims=NN):
    return lax.dot_general(a, b, dims, preferred_element_type=F32)


def split(a):
    high = a.astype(BF16)
    return high, (a - high.astype(F32)).astype(BF16)


def build_tables(prm_ref, phi, plo, qhi, qlo, thi, tlo, bas):
    prm = prm_ref[...]
    row = lambda k: prm[k : k + 1, :]
    col = lambda k: jnp.broadcast_to(row(k), (LANES, LANES)).T
    d_row, f_row = row(0), row(1)
    d_col, f_col, r_col = col(0), col(1), col(2)
    lane = lax.broadcasted_iota(jnp.int32, (LANES, TOK), 1)
    sub = lax.broadcasted_iota(jnp.int32, (LANES, TOK), 0)
    t_q = (lane + 1).astype(F32)
    t_b = lane.astype(F32)
    t_p = (TOK - 1 - sub).astype(F32)
    mag = jnp.exp(-d_col * t_q)
    ang = f_col * t_q
    q_re, q_im = mag * jnp.cos(ang), mag * jnp.sin(ang)
    basis = jnp.exp(-d_col * t_b) * jnp.cos(f_col * t_b)
    bas[...] = basis
    mag = jnp.exp(-d_row * t_p)
    ang = f_row * t_p
    p_re, p_im = mag * jnp.cos(ang), mag * jnp.sin(ang)
    filt = jnp.sum((r_col * basis).reshape(CB, ORDER, TOK), axis=1)
    for c in range(CB):
        cols = slice(c * TOK, (c + 1) * TOK)
        own = lane // ORDER == c
        high, low = split(
            jnp.concatenate([jnp.where(own, p_re, 0.0), jnp.where(own, p_im, 0.0)], axis=1)
        )
        phi[cols, :] = high
        plo[cols, :] = low
        own = sub // ORDER == c
        high, low = split(
            jnp.concatenate([jnp.where(own, q_re, 0.0), jnp.where(own, q_im, 0.0)], axis=0)
        )
        qhi[:, cols] = high
        qlo[:, cols] = low
        rolled = pltpu.roll(
            jnp.broadcast_to(filt[c : c + 1, :], (TOK, TOK)), 0, 1, stride=1, stride_axis=0
        )
        skip = prm[3:4, c * ORDER : c * ORDER + 1]
        toep = jnp.where(lane >= sub, rolled, 0.0) + jnp.where(lane == sub, skip, 0.0)
        high, low = split(toep)
        thi[c] = high
        tlo[c] = low


def scan_chunks(re, im, lam, forward):
    at = lax.broadcasted_iota(jnp.int32, re.shape, 0)

    def shift(a, by):
        if forward:
            return jnp.where(at >= by, pltpu.roll(a, by, 0), 0.0)
        return jnp.where(at < NCTX - by, pltpu.roll(a, NCTX - by, 0), 0.0)

    re, im = shift(re, 1), shift(im, 1)
    by = 1
    for l_re, l_im in lam:
        s_re, s_im = shift(re, by), shift(im, by)
        re, im = re + l_re * s_re - l_im * s_im, im + l_re * s_im + l_im * s_re
        by *= 2
    return re, im


def convolve(prm_ref, x32, y32, phi, plo, qhi, qlo, thi, tlo, bas, res_ref):
    prm = prm_ref[...]
    d_row, f_row, r_row = prm[0:1, :], prm[1:2, :], prm[2:3, :]
    lam = []
    for k in range(6):
        span = float(TOK * 2**k)
        mag = jnp.exp(-d_row * span)
        lam.append((mag * jnp.cos(f_row * span), mag * jnp.sin(f_row * span)))
    xs = [x32[pl.ds(c, NCTX, stride=2 * CB), :].astype(BF16) for c in range(CB)]
    gs = [x32[pl.ds(CB + c, NCTX, stride=2 * CB), :].astype(BF16) for c in range(CB)]
    xcat = jnp.concatenate(xs, axis=1)
    gcat = jnp.concatenate(gs, axis=1)
    e = dot(xcat, phi[...]) + dot(xcat, plo[...])
    f = dot(gcat, qhi[...], NT) + dot(gcat, qlo[...], NT)
    h_re, h_im = scan_chunks(e[:, :LANES], e[:, LANES:], lam, True)
    k_re, k_im = scan_chunks(f[:, :LANES], f[:, LANES:], lam, False)
    across = jnp.sum(h_re * f[:, :LANES] - h_im * f[:, LANES:], axis=0, keepdims=True)
    hh, hl = split(jnp.concatenate([r_row * h_re, -r_row * h_im], axis=1))
    kh, kl = split(jnp.concatenate([r_row * k_re, -r_row * k_im], axis=1))
    y = dot(hh, qhi[...]) + dot(hl, qhi[...]) + dot(hh, qlo[...])
    z = dot(kh, phi[...], NT) + dot(kl, phi[...], NT) + dot(kh, plo[...], NT)
    lane = lax.broadcasted_iota(jnp.int32, (TOK, TOK), 1)
    sub = lax.broadcasted_iota(jnp.int32, (TOK, TOK), 0)
    flip = jnp.where(lane + sub == TOK - 1, 1.0, 0.0).astype(BF16)
    corr = []
    for c in range(CB):
        cols = slice(c * TOK, (c + 1) * TOK)
        yc = y[:, cols] + dot(xs[c], thi[c]) + dot(xs[c], tlo[c])
        zc = z[:, cols] + dot(gs[c], thi[c], NT) + dot(gs[c], tlo[c], NT)
        y32[pl.ds(c, NCTX, stride=2 * CB), :] = yc
        y32[pl.ds(CB + c, NCTX, stride=2 * CB), :] = zc
        back_t = dot(xs[c], flip).T.astype(BF16)
        pairs = dot(back_t, gs[c])
        lagged = pltpu.roll(pairs, 1, 1, stride=1, stride_axis=0)
        corr.append(jnp.sum(jnp.where(lane <= sub, lagged, 0.0), axis=0, keepdims=True))
    spread = jnp.concatenate([jnp.broadcast_to(a, (ORDER, TOK)) for a in corr], axis=0)
    within = jnp.sum((spread * bas[...]).T, axis=0, keepdims=True)
    res_ref[...] = jnp.broadcast_to(within + across, res_ref.shape)


def kernel(
    f_ref,
    g_ref,
    wv_ref,
    wq_ref,
    wo_ref,
    prm_ref,
    mixed_ref,
    gin_ref,
    res_ref,
    w,
    acc,
    query,
    gg,
    snd,
    rcv,
    snd2,
    rcv2,
    x32,
    y32,
    phi,
    plo,
    qhi,
    qlo,
    thi,
    tlo,
    bas,
    part,
    got,
    ssem,
    rsem,
    xsem,
    psem,
):
    ctx = lax.axis_index("ctx")
    tp = lax.axis_index("tp")
    xy = ctx // NZ
    x, y, z = xy // NY, xy % NY, ctx % NZ
    xl, xr = (x + NX - 1) % NX, (x + 1) % NX
    zl, zr = (z + NZ - 1) % NZ, (z + 1) % NZ
    yo = 1 - y

    barrier = pltpu.get_barrier_semaphore()

    def greet_ctx(k, carry):
        pl.semaphore_signal(
            barrier, inc=1, device_id=((ctx + k) % NCTX, tp), device_id_type=MESH
        )
        return carry

    def greet_tp(k, carry):
        pl.semaphore_signal(barrier, inc=1, device_id=(ctx, (tp + k) % NTP), device_id_type=MESH)
        return carry

    lax.fori_loop(1, NCTX, greet_ctx, 0)
    lax.fori_loop(1, NTP, greet_tp, 0)
    for i, ref in enumerate((wv_ref, wq_ref, wo_ref)):
        w[i, xy, z] = ref[...]
    pl.semaphore_wait(barrier, NCTX + NTP - 2)

    def dev(xi, yi, zi):
        return ((xi * NY + yi) * NZ + zi, tp)

    def copy(half, i, k, ref, device):
        return pltpu.make_async_remote_copy(
            src_ref=ref,
            dst_ref=ref,
            send_sem=ssem.at[half, i, k],
            recv_sem=rsem.at[half, i, k],
            device_id=device,
            device_id_type=MESH,
        )

    to_y, to_r, to_l = dev(x, yo, z), dev(xr, y, z), dev(xl, y, z)
    to_u, to_d = dev(x, y, zr), dev(x, y, zl)

    first, second = pl.ds(0, HALF), pl.ds(HALF, HALF)
    a_own = lambda i, yi: w.at[i, x * NY + yi, z, first]
    a_pair = lambda i, xi: w.at[i, pl.ds(xi * NY, NY), z, first]
    a_one = lambda i, xi, yi: w.at[i, xi * NY + yi, z, first]

    def a_plane(i, step, up, whole):
        zi = (z + NZ - step) % NZ if up else (z + step) % NZ
        if whole:
            return w.at[i, :, zi, first]
        return w.at[i, pl.ds(0 if up else NX, NX), zi, first]

    def b_block(i, step, up, whole):
        zi = (z + NZ - step) % NZ if up else (z + step) % NZ
        rows = second if whole else pl.ds(HALF if up else HALF + HALF // 2, HALF // 2)
        return w.at[i, xy, zi, rows]

    b_line = lambda i, yi: w.at[i, x * NY + yi, :, second]
    b_pair = lambda i, xi: w.at[i, pl.ds(xi * NY, NY), :, second]
    b_one = lambda i, xi, yi: w.at[i, xi * NY + yi, :, second]
    x2 = (x + 2) % NX

    def a_copy(i, k):
        if k == 0:
            return a_own(i, y), to_y, a_own(i, yo)
        if k == 1:
            return a_pair(i, x), to_r, a_pair(i, xl)
        if k == 2:
            return a_pair(i, x), to_l, a_pair(i, xr)
        if k == 3:
            return a_one(i, xl, 0), to_r, a_one(i, x2, 0)
        if k == 4:
            return a_one(i, xr, 1), to_l, a_one(i, x2, 1)
        up, step = k < 9, (k - 5) % 4
        whole = step < 3
        return a_plane(i, step, up, whole), to_u if up else to_d, a_plane(i, step + 1, up, whole)

    def b_copy(i, k):
        if k == 8:
            return b_line(i, y), to_y, b_line(i, yo)
        if k == 9:
            return b_pair(i, x), to_r, b_pair(i, xl)
        if k == 10:
            return b_pair(i, x), to_l, b_pair(i, xr)
        if k == 11:
            return b_one(i, xl, 0), to_r, b_one(i, x2, 0)
        if k == 12:
            return b_one(i, xr, 1), to_l, b_one(i, x2, 1)
        up, step = k < 4, k % 4
        whole = step < 3
        return b_block(i, step, up, whole), to_u if up else to_d, b_block(i, step + 1, up, whole)

    makers = (a_copy, b_copy)

    def start(half, i, *ks):
        for k in ks:
            out, device, _ = makers[half](i, k)
            copy(half, i, k, out, device).start()

    def arrive(half, i, *ks):
        for k in ks:
            _, device, incoming = makers[half](i, k)
            copy(half, i, k, incoming, device).wait_recv()

    every = range(3)
    for i in every:
        start(0, i, 0)
        start(1, i, 0, 4)
    for i in every:
        arrive(0, i, 0)
        start(0, i, 1, 2)
        arrive(1, i, 0, 4)
        start(1, i, 1, 5)
    for i in every:
        arrive(0, i, 1)
        start(0, i, 3)
        arrive(0, i, 2)
        start(0, i, 4)
        arrive(1, i, 1, 5)
        start(1, i, 2, 6)
    for i in every:
        arrive(0, i, 3, 4)
        start(0, i, 5, 9)
        arrive(1, i, 2, 6)
        start(1, i, 3, 7)
    build_tables(prm_ref, phi, plo, qhi, qlo, thi, tlo, bas)
    for i in every:
        arrive(1, i, 3, 7)
        start(1, i, 8)

    def a_next(i, step):
        arrive(0, i, 5 + step, 9 + step)
        start(0, i, 6 + step, 10 + step)

    def b_first(i):
        arrive(1, i, 8)
        start(1, i, 9, 10)

    def b_second(i):
        arrive(1, i, 9)
        start(1, i, 11)
        arrive(1, i, 10)
        start(1, i, 12)

    a_next(0, 0)
    b_first(0)
    a_next(1, 0)
    b_first(1)
    a_next(2, 0)
    b_first(2)
    b_second(0)
    a_next(0, 1)
    a_next(1, 1)
    b_second(1)
    a_next(2, 1)
    a_next(0, 2)
    b_second(2)
    a_next(1, 2)
    a_next(2, 2)

    def project(lhs_ref, i):
        acc[...] = jnp.zeros_like(acc)

        def step(kb, carry):
            cols = pl.ds(pl.multiple_of(kb * CG, CG), CG)
            acc[...] += dot(lhs_ref[:, cols], w[i, kb].reshape(CG, CG))
            return carry

        lax.fori_loop(0, NCTX // NZ, step, 0)

    def finish(i):
        arrive(0, i, 8, 12)
        arrive(1, i, 11, 12)

    finish(0)
    project(f_ref, 0)
    value_t = acc[...].T.reshape(NCTX, CB, TOK)
    x32[...] = jnp.concatenate([value_t, value_t], axis=1).reshape(x32.shape)
    finish(1)
    project(f_ref, 1)
    query[...] = acc[...].astype(BF16).astype(F32)
    finish(2)
    project(g_ref, 2)
    gg[...] = acc[...]
    grad_t = (acc[...] * query[...]).T.reshape(NCTX, CB, TOK)
    both = jnp.concatenate([x32[...].reshape(NCTX, 2 * CB, TOK)[:, :CB], grad_t], axis=1)
    snd[...] = both.astype(BF16)

    def exchange(src, dst, which):
        def one(k, carry):
            to = (ctx + k) % NCTX
            pltpu.make_async_remote_copy(
                src_ref=src.at[to],
                dst_ref=dst.at[ctx],
                send_sem=xsem.at[which, 0],
                recv_sem=xsem.at[which, 1],
                device_id=(to, tp),
                device_id_type=MESH,
            ).start()
            return carry

        lax.fori_loop(1, NCTX, one, 0)
        dst[ctx] = src[ctx]
        rest = dst.at[pl.ds(0, NCTX - 1)]
        pltpu.make_async_copy(rest, rest, xsem.at[which, 1]).wait()

    def sent(src, which):
        rest = src.at[pl.ds(0, NCTX - 1)]
        pltpu.make_async_copy(rest, rest, xsem.at[which, 0]).wait()

    exchange(snd, rcv, 0)
    x32[...] = rcv[...].astype(F32).reshape(x32.shape)
    convolve(prm_ref, x32, y32, phi, plo, qhi, qlo, thi, tlo, bas, res_ref)
    snd2[...] = y32[...].reshape(snd2.shape).astype(BF16)
    exchange(snd2, rcv2, 1)

    back = rcv2[...].astype(F32)
    state = back[:, :CB].reshape(CG, TOK).T
    grad_value = back[:, CB:].reshape(CG, TOK).T.astype(BF16)
    gated = (query[...] * state).astype(BF16)
    grad_query = (gg[...] * state).astype(BF16)

    def scatter(which, block):
        def one(k, carry):
            to = (tp + k) % NTP
            part[which, to] = block(to).astype(BF16)

            @pl.when(k < NTP)
            def _():
                pltpu.make_async_remote_copy(
                    src_ref=part.at[which, to],
                    dst_ref=got.at[which, tp],
                    send_sem=psem.at[which, 0],
                    recv_sem=psem.at[which, 1],
                    device_id=(ctx, to),
                    device_id_type=MESH,
                ).start()

            return carry

        lax.fori_loop(1, NTP + 1, one, 0)
        got[which, tp] = part[which, tp]

    def collect(which, out):
        rest = got.at[which, pl.ds(0, NTP - 1)]
        pltpu.make_async_copy(rest, rest, psem.at[which, 1]).wait()
        total = got[which, 0].astype(F32)
        for k in range(1, NTP):
            total += got[which, k].astype(F32)
        out[...] = total.astype(BF16)

    scatter(0, lambda q: dot(gated, w[2, q].reshape(CG, CG), NT))
    scatter(
        1,
        lambda q: dot(grad_query, w[1, q].reshape(CG, CG), NT)
        + dot(grad_value, w[0, q].reshape(CG, CG), NT),
    )
    collect(0, mixed_ref)
    collect(1, gin_ref)

    sent(snd, 0)
    sent(snd2, 1)
    for which in range(2):
        rest = part.at[which, pl.ds(0, NTP - 1)]
        pltpu.make_async_copy(rest, rest, psem.at[which, 0]).wait()
    for half in range(2):
        for i in every:
            for k in range(NK):
                out, device, _ = makers[half](i, k)
                copy(half, i, k, out, device).wait_send()


def body(features, grad_out, w_value, w_query, w_out, residues, decays, freqs, skips):
    first = lax.axis_index("ctx") * CB
    own = lambda a: lax.dynamic_slice_in_dim(a, first, CB, a.ndim - 1)
    flat = lambda a: own(a).T.reshape(1, LANES)
    skip_row = jnp.broadcast_to(own(skips)[:, None], (CB, ORDER)).reshape(1, LANES)
    prm = jnp.concatenate(
        [flat(decays), flat(freqs), flat(residues), skip_row, jnp.zeros((4, LANES), F32)], axis=0
    )
    vmem = pl.BlockSpec(memory_space=pltpu.VMEM)
    scratch = [
        pltpu.VMEM((3, NX * NY, NZ, ROWS, CG), BF16),
        pltpu.VMEM((TOK, CG), F32),
        pltpu.VMEM((TOK, CG), F32),
        pltpu.VMEM((TOK, CG), F32),
        pltpu.VMEM((NCTX, 2 * CB, TOK), BF16),
        pltpu.VMEM((NCTX, 2 * CB, TOK), BF16),
        pltpu.VMEM((NCTX, 2 * CB, TOK), BF16),
        pltpu.VMEM((NCTX, 2 * CB, TOK), BF16),
        pltpu.VMEM((NCTX * 2 * CB, TOK), F32),
        pltpu.VMEM((NCTX * 2 * CB, TOK), F32),
        pltpu.VMEM((CB * TOK, 2 * LANES), BF16),
        pltpu.VMEM((CB * TOK, 2 * LANES), BF16),
        pltpu.VMEM((2 * LANES, CB * TOK), BF16),
        pltpu.VMEM((2 * LANES, CB * TOK), BF16),
        pltpu.VMEM((CB, TOK, TOK), BF16),
        pltpu.VMEM((CB, TOK, TOK), BF16),
        pltpu.VMEM((LANES, TOK), F32),
        pltpu.VMEM((2, NTP, TOK, CG), BF16),
        pltpu.VMEM((2, NTP, TOK, CG), BF16),
        pltpu.SemaphoreType.DMA((2, 3, NK)),
        pltpu.SemaphoreType.DMA((2, 3, NK)),
        pltpu.SemaphoreType.DMA((2, 2)),
        pltpu.SemaphoreType.DMA((2, 2)),
    ]
    mixed, grad_in, res = pl.pallas_call(
        kernel,
        out_shape=(
            jax.ShapeDtypeStruct((TOK, CG), BF16),
            jax.ShapeDtypeStruct((TOK, CG), BF16),
            jax.ShapeDtypeStruct((8, LANES), F32),
        ),
        in_specs=[vmem] * 6,
        out_specs=(vmem,) * 3,
        scratch_shapes=scratch,
        compiler_params=pltpu.CompilerParams(
            collective_id=0, has_side_effects=True, vmem_limit_bytes=48 * 2**20
        ),
        cost_estimate=pl.CostEstimate(
            flops=2 * 6 * TOK * CG * 4096, bytes_accessed=2**22, transcendentals=2**17
        ),
    )(features, grad_out, w_value, w_query, w_out.T, prm)
    return mixed, grad_in, res[0].reshape(CB, ORDER).T


def solution(mesh):
    placed = (
        P("ctx", None),
        P("ctx", None),
        P("ctx", "tp"),
        P("ctx", "tp"),
        P("tp", "ctx"),
        P(None, "tp"),
        P(None, "tp"),
        P(None, "tp"),
        P("tp"),
    )
    return jax.shard_map(
        body,
        mesh=mesh,
        in_specs=placed,
        out_specs=(P("ctx", "tp"), P("ctx", "tp"), P(None, ("tp", "ctx"))),
        check_vma=False,
    )
```

```python
import functools

import jax
import jax.numpy as jnp
from jax import lax
from jax.experimental import pallas as pl
from jax.experimental.pallas import tpu as pltpu
from jax.sharding import PartitionSpec as P

MESH = pl.DeviceIdType.MESH
F32, BF16 = jnp.float32, jnp.bfloat16
NX, NY, NZ = 4, 2, 8
NCTX, NTP = 64, 8
ROWS = 64
HALF = ROWS // 2
CG = 512
TOK = 128
CB = 8
ORDER = 16
LANES = CB * ORDER
NK = 12

NN = (((1,), (0,)), ((), ()))
NT = (((1,), (1,)), ((), ()))


def dot(a, b, dims=NN):
    return lax.dot_general(a, b, dims, preferred_element_type=F32)


def split(a):
    high = a.astype(BF16)
    return high, (a - high.astype(F32)).astype(BF16)


def build_tables(prm_ref, phi, plo, qhi, qlo, thi, tlo, bas):
    prm = prm_ref[...]
    row = lambda k: prm[k : k + 1, :]
    col = lambda k: jnp.broadcast_to(row(k), (LANES, LANES)).T
    d_row, f_row = row(0), row(1)
    d_col, f_col, r_col = col(0), col(1), col(2)
    lane = lax.broadcasted_iota(jnp.int32, (LANES, TOK), 1)
    sub = lax.broadcasted_iota(jnp.int32, (LANES, TOK), 0)
    t_q = (lane + 1).astype(F32)
    t_b = lane.astype(F32)
    t_p = (TOK - 1 - sub).astype(F32)
    mag = jnp.exp(-d_col * t_q)
    ang = f_col * t_q
    q_re, q_im = mag * jnp.cos(ang), mag * jnp.sin(ang)
    basis = jnp.exp(-d_col * t_b) * jnp.cos(f_col * t_b)
    bas[...] = basis
    mag = jnp.exp(-d_row * t_p)
    ang = f_row * t_p
    p_re, p_im = mag * jnp.cos(ang), mag * jnp.sin(ang)
    filt = jnp.sum((r_col * basis).reshape(CB, ORDER, TOK), axis=1)
    for c in range(CB):
        cols = slice(c * TOK, (c + 1) * TOK)
        own = lane // ORDER == c
        high, low = split(
            jnp.concatenate([jnp.where(own, p_re, 0.0), jnp.where(own, p_im, 0.0)], axis=1)
        )
        phi[cols, :] = high
        plo[cols, :] = low
        own = sub // ORDER == c
        high, low = split(
            jnp.concatenate([jnp.where(own, q_re, 0.0), jnp.where(own, q_im, 0.0)], axis=0)
        )
        qhi[:, cols] = high
        qlo[:, cols] = low
        rolled = pltpu.roll(
            jnp.broadcast_to(filt[c : c + 1, :], (TOK, TOK)), 0, 1, stride=1, stride_axis=0
        )
        skip = prm[3:4, c * ORDER : c * ORDER + 1]
        toep = jnp.where(lane >= sub, rolled, 0.0) + jnp.where(lane == sub, skip, 0.0)
        high, low = split(toep)
        thi[c] = high
        tlo[c] = low


def scan_chunks(re, im, lam, forward):
    at = lax.broadcasted_iota(jnp.int32, re.shape, 0)

    def shift(a, by):
        if forward:
            return jnp.where(at >= by, pltpu.roll(a, by, 0), 0.0)
        return jnp.where(at < NCTX - by, pltpu.roll(a, NCTX - by, 0), 0.0)

    re, im = shift(re, 1), shift(im, 1)
    by = 1
    for l_re, l_im in lam:
        s_re, s_im = shift(re, by), shift(im, by)
        re, im = re + l_re * s_re - l_im * s_im, im + l_re * s_im + l_im * s_re
        by *= 2
    return re, im


def convolve(prm_ref, x32, y32, phi, plo, qhi, qlo, thi, tlo, bas, res_ref):
    prm = prm_ref[...]
    d_row, f_row, r_row = prm[0:1, :], prm[1:2, :], prm[2:3, :]
    lam = []
    for k in range(6):
        span = float(TOK * 2**k)
        mag = jnp.exp(-d_row * span)
        lam.append((mag * jnp.cos(f_row * span), mag * jnp.sin(f_row * span)))
    xs = [x32[pl.ds(c, NCTX, stride=2 * CB), :].astype(BF16) for c in range(CB)]
    gs = [x32[pl.ds(CB + c, NCTX, stride=2 * CB), :].astype(BF16) for c in range(CB)]
    xcat = jnp.concatenate(xs, axis=1)
    gcat = jnp.concatenate(gs, axis=1)
    e = dot(xcat, phi[...]) + dot(xcat, plo[...])
    f = dot(gcat, qhi[...], NT) + dot(gcat, qlo[...], NT)
    h_re, h_im = scan_chunks(e[:, :LANES], e[:, LANES:], lam, True)
    k_re, k_im = scan_chunks(f[:, :LANES], f[:, LANES:], lam, False)
    across = jnp.sum(h_re * f[:, :LANES] - h_im * f[:, LANES:], axis=0, keepdims=True)
    hh, hl = split(jnp.concatenate([r_row * h_re, -r_row * h_im], axis=1))
    kh, kl = split(jnp.concatenate([r_row * k_re, -r_row * k_im], axis=1))
    y = dot(hh, qhi[...]) + dot(hl, qhi[...]) + dot(hh, qlo[...])
    z = dot(kh, phi[...], NT) + dot(kl, phi[...], NT) + dot(kh, plo[...], NT)
    lane = lax.broadcasted_iota(jnp.int32, (TOK, TOK), 1)
    sub = lax.broadcasted_iota(jnp.int32, (TOK, TOK), 0)
    flip = jnp.where(lane + sub == TOK - 1, 1.0, 0.0).astype(BF16)
    corr = []
    for c in range(CB):
        cols = slice(c * TOK, (c + 1) * TOK)
        yc = y[:, cols] + dot(xs[c], thi[c]) + dot(xs[c], tlo[c])
        zc = z[:, cols] + dot(gs[c], thi[c], NT) + dot(gs[c], tlo[c], NT)
        y32[pl.ds(c, NCTX, stride=2 * CB), :] = yc
        y32[pl.ds(CB + c, NCTX, stride=2 * CB), :] = zc
        back_t = dot(xs[c], flip).T.astype(BF16)
        pairs = dot(back_t, gs[c])
        lagged = pltpu.roll(pairs, 1, 1, stride=1, stride_axis=0)
        corr.append(jnp.sum(jnp.where(lane <= sub, lagged, 0.0), axis=0, keepdims=True))
    spread = jnp.concatenate([jnp.broadcast_to(a, (ORDER, TOK)) for a in corr], axis=0)
    within = jnp.sum((spread * bas[...]).T, axis=0, keepdims=True)
    res_ref[...] = jnp.broadcast_to(within + across, res_ref.shape)


def kernel(
    f_ref,
    g_ref,
    wv_ref,
    wq_ref,
    wo_ref,
    prm_ref,
    mixed_ref,
    gin_ref,
    res_ref,
    w,
    lhs,
    acc,
    own,
    psnd,
    prcv,
    query,
    gg,
    snd,
    rcv,
    snd2,
    rcv2,
    x32,
    y32,
    phi,
    plo,
    qhi,
    qlo,
    thi,
    tlo,
    bas,
    pair,
    part,
    sib,
    summed,
    got,
    ssem,
    rsem,
    lsem,
    fsem,
    ysem,
    xsem,
    csem,
    psem,
):
    ctx = lax.axis_index("ctx")
    tp = lax.axis_index("tp")
    xy = ctx // NZ
    x, y, z = xy // NY, xy % NY, ctx % NZ
    y_hi, core = tp // 2, tp % 2
    xl, xr, x2 = (x + NX - 1) % NX, (x + 1) % NX, (x + 2) % NX
    zl, zr = (z + NZ - 1) % NZ, (z + 1) % NZ
    yo = 1 - y
    at = lambda xi, yi, zi: (xi * NY + yi) * NZ + zi
    partner = (at(x, yo, z), tp)
    sibling = (ctx, y_hi * 2 + 1 - core)
    sum_ctx = at(x, core, z)
    to_self = core == y

    barrier = pltpu.get_barrier_semaphore()

    def greet(device):
        pl.semaphore_signal(barrier, inc=1, device_id=device, device_id_type=MESH)

    def greet_ctx(k, carry):
        greet(((ctx + k) % NCTX, tp))
        return carry

    lax.fori_loop(1, NCTX, greet_ctx, 0)
    greet(sibling)
    for k in range(1, NX):
        greet((sum_ctx, (y_hi + k) % NX * 2 + y))

    @pl.when(jnp.logical_not(to_self))
    def _():
        greet((sum_ctx, y_hi * 2 + y))

    def columns(block):
        return pl.ds(pl.multiple_of(block * CG, CG), CG)

    def token_rows(yi):
        return pl.ds(pl.multiple_of(yi * TOK, TOK), TOK)

    for i, ref in enumerate((wv_ref, wq_ref, wo_ref)):
        w[i, x, z] = ref[...]
    for a, ref in enumerate((f_ref, g_ref)):
        for b in range(NX):
            pltpu.make_async_copy(
                ref.at[:, columns(b * NY + y)], lhs.at[a, b, token_rows(y)], lsem.at[a, b]
            ).start()
    pl.semaphore_wait(barrier, NCTX - 1 + 1 + NX - 1 + jnp.where(to_self, 0, 1))

    def swap(a, b):
        return pltpu.make_async_remote_copy(
            src_ref=(f_ref, g_ref)[a].at[:, columns(b * NY + yo)],
            dst_ref=lhs.at[a, b, token_rows(y)],
            send_sem=fsem.at[0, a, b],
            recv_sem=fsem.at[1, a, b],
            device_id=partner,
            device_id_type=MESH,
        )

    for a in range(2):
        for b in range(NX):
            swap(a, b).start()

    def copy(half, i, k, ref, device):
        return pltpu.make_async_remote_copy(
            src_ref=ref,
            dst_ref=ref,
            send_sem=ssem.at[half, i, k],
            recv_sem=rsem.at[half, i, k],
            device_id=device,
            device_id_type=MESH,
        )

    to_r, to_l = (at(xr, y, z), tp), (at(xl, y, z), tp)
    to_u, to_d = (at(x, y, zr), tp), (at(x, y, zl), tp)
    quarter = HALF // 2
    first, second = pl.ds(0, HALF), pl.ds(HALF, HALF)

    def z_from(step, up):
        return (z + NZ - step) % NZ if up else (z + step) % NZ

    def a_copy(i, k):
        if k < 2:
            return w.at[i, x, z, first], (to_r, to_l)[k], w.at[i, (xl, xr)[k], z, first]
        if k < 4:
            rows = pl.ds((k - 2) * quarter, quarter)
            return w.at[i, (xl, xr)[k - 2], z, rows], (to_r, to_l)[k - 2], w.at[i, x2, z, rows]
        up, step = k < 8, k % 4
        some = slice(None) if step < 3 else pl.ds(0 if up else NX // 2, NX // 2)
        return (
            w.at[i, some, z_from(step, up), first],
            to_u if up else to_d,
            w.at[i, some, z_from(step + 1, up), first],
        )

    def b_copy(i, k):
        if k < 8:
            up, step = k < 4, k % 4
            rows = second if step < 3 else pl.ds(HALF if up else HALF + quarter, quarter)
            return (
                w.at[i, x, z_from(step, up), rows],
                to_u if up else to_d,
                w.at[i, x, z_from(step + 1, up), rows],
            )
        if k < 10:
            return w.at[i, x, :, second], (to_r, to_l)[k - 8], w.at[i, (xl, xr)[k - 8], :, second]
        some = pl.ds((k - 10) * (NZ // 2), NZ // 2)
        return (
            w.at[i, (xl, xr)[k - 10], some, second],
            (to_r, to_l)[k - 10],
            w.at[i, x2, some, second],
        )

    makers = (a_copy, b_copy)

    def start(half, i, *ks):
        for k in ks:
            out, device, _ = makers[half](i, k)
            copy(half, i, k, out, device).start()

    def arrive(half, i, *ks):
        for k in ks:
            _, device, incoming = makers[half](i, k)
            copy(half, i, k, incoming, device).wait_recv()

    every = range(3)
    for i in every:
        start(0, i, 0, 1)
        start(1, i, 0, 4)
    for i in every:
        arrive(0, i, 0)
        start(0, i, 2)
        arrive(0, i, 1)
        start(0, i, 3)
        arrive(1, i, 0, 4)
        start(1, i, 1, 5)
    for i in every:
        arrive(0, i, 2, 3)
        start(0, i, 4, 8)
        arrive(1, i, 1, 5)
        start(1, i, 2, 6)
    for i in every:
        arrive(1, i, 2, 6)
        start(1, i, 3, 7)
    for i in every:
        arrive(1, i, 3, 7)
        start(1, i, 8, 9)

    def a_next(i, step):
        arrive(0, i, 4 + step, 8 + step)
        start(0, i, 5 + step, 9 + step)

    def b_second(i):
        arrive(1, i, 8)
        start(1, i, 10)
        arrive(1, i, 9)
        start(1, i, 11)

    for i in every:
        a_next(i, 0)
    build_tables(prm_ref, phi, plo, qhi, qlo, thi, tlo, bas)
    b_second(0)
    a_next(0, 1)
    a_next(1, 1)
    b_second(1)
    a_next(2, 1)
    a_next(0, 2)
    b_second(2)
    a_next(1, 2)
    a_next(2, 2)

    def give(i):
        return pltpu.make_async_remote_copy(
            src_ref=psnd.at[i],
            dst_ref=prcv.at[i],
            send_sem=ysem.at[0, i],
            recv_sem=ysem.at[1, i],
            device_id=partner,
            device_id_type=MESH,
        )

    def project(a, i):
        acc[...] = jnp.zeros_like(acc)

        def step(b, carry):
            acc[...] += dot(lhs[a, b], w[i, b].reshape(CG, CG))
            return carry

        lax.fori_loop(0, NX, step, 0)
        psnd[i] = acc[token_rows(yo), :].astype(BF16)
        give(i).start()
        own[i] = acc[token_rows(y), :]

    def rows_in(a):
        for b in range(NX):
            pltpu.make_async_copy(
                (f_ref, g_ref)[a].at[:, columns(b * NY + y)],
                lhs.at[a, b, token_rows(y)],
                lsem.at[a, b],
            ).wait()
            swap(a, b).wait_recv()

    def finish(i):
        arrive(0, i, 7, 11)
        arrive(1, i, 10, 11)

    def total(i):
        give(i).wait_recv()
        return own[i] + prcv[i].astype(F32)

    rows_in(0)
    finish(0)
    project(0, 0)
    finish(1)
    project(0, 1)
    value_t = total(0).T.reshape(NCTX, CB, TOK)
    x32[...] = jnp.concatenate([value_t, value_t], axis=1).reshape(x32.shape)
    rows_in(1)
    finish(2)
    project(1, 2)
    query[...] = total(1).astype(BF16).astype(F32)
    gg[...] = total(2)
    grad_t = (gg[...] * query[...]).T.reshape(NCTX, CB, TOK)
    both = jnp.concatenate([x32[...].reshape(NCTX, 2 * CB, TOK)[:, :CB], grad_t], axis=1)
    snd[...] = both.astype(BF16)

    def exchange(src, dst, which):
        def one(k, carry):
            to = (ctx + k) % NCTX
            pltpu.make_async_remote_copy(
                src_ref=src.at[to],
                dst_ref=dst.at[ctx],
                send_sem=xsem.at[which, 0],
                recv_sem=xsem.at[which, 1],
                device_id=(to, tp),
                device_id_type=MESH,
            ).start()
            return carry

        lax.fori_loop(1, NCTX, one, 0)
        dst[ctx] = src[ctx]
        rest = dst.at[pl.ds(0, NCTX - 1)]
        pltpu.make_async_copy(rest, rest, xsem.at[which, 1]).wait()

    def sent(src, which):
        rest = src.at[pl.ds(0, NCTX - 1)]
        pltpu.make_async_copy(rest, rest, xsem.at[which, 0]).wait()

    exchange(snd, rcv, 0)
    x32[...] = rcv[...].astype(F32).reshape(x32.shape)
    convolve(prm_ref, x32, y32, phi, plo, qhi, qlo, thi, tlo, bas, res_ref)
    snd2[...] = y32[...].reshape(snd2.shape).astype(BF16)
    exchange(snd2, rcv2, 1)

    def share(i):
        return pltpu.make_async_remote_copy(
            src_ref=pair.at[i, token_rows(y)],
            dst_ref=pair.at[i, token_rows(y)],
            send_sem=ysem.at[0, 3 + i],
            recv_sem=ysem.at[1, 3 + i],
            device_id=partner,
            device_id_type=MESH,
        )

    def shared(i):
        return pltpu.make_async_remote_copy(
            src_ref=pair.at[i, token_rows(yo)],
            dst_ref=pair.at[i, token_rows(yo)],
            send_sem=ysem.at[0, 3 + i],
            recv_sem=ysem.at[1, 3 + i],
            device_id=partner,
            device_id_type=MESH,
        )

    back = rcv2[...].astype(F32)
    state = back[:, :CB].reshape(CG, TOK).T
    pair[0, token_rows(y), :] = (query[...] * state).astype(BF16)
    share(0).start()
    pair[1, token_rows(y), :] = (gg[...] * state).astype(BF16)
    share(1).start()
    pair[2, token_rows(y), :] = back[:, CB:].reshape(CG, TOK).T.astype(BF16)
    share(2).start()

    def to_sibling(which, b):
        return pltpu.make_async_remote_copy(
            src_ref=part.at[which, b],
            dst_ref=sib.at[which, b],
            send_sem=csem.at[0, which, b],
            recv_sem=csem.at[1, which, b],
            device_id=sibling,
            device_id_type=MESH,
        )

    def onward(which, b):
        return pltpu.make_async_remote_copy(
            src_ref=summed.at[which, b],
            dst_ref=got.at[which, y_hi],
            send_sem=psem.at[0, which, b],
            recv_sem=psem.at[1, which, y_hi],
            device_id=(sum_ctx, b * 2 + y),
            device_id_type=MESH,
        )

    def at_home(which):
        return pltpu.make_async_copy(
            summed.at[which, y_hi], got.at[which, y_hi], psem.at[1, which, y_hi]
        )

    def scatter(which, block):
        def give_half(k, carry):
            b = (y_hi + k) % NX
            part[which, b] = block(token_rows(1 - core), b).astype(BF16)
            to_sibling(which, b).start()
            return carry

        def send_on(k, carry):
            b = (y_hi + k) % NX
            mine = block(token_rows(core), b)
            to_sibling(which, b).wait_recv()
            summed[which, b] = (mine + sib[which, b].astype(F32)).astype(BF16)
            home = jnp.logical_and(to_self, b == y_hi)

            @pl.when(home)
            def _():
                at_home(which).start()

            @pl.when(jnp.logical_not(home))
            def _():
                onward(which, b).start()

            return carry

        lax.fori_loop(1, NX + 1, give_half, 0)
        lax.fori_loop(1, NX + 1, send_on, 0)

    def collect(which, out):
        total = None
        for k in range(NX):
            pltpu.make_async_copy(got.at[which, k], got.at[which, k], psem.at[1, which, k]).wait()
            term = got[which, k].astype(F32)
            total = term if k == 0 else total + term
        out[...] = total.astype(BF16)

    shared(0).wait_recv()
    scatter(0, lambda rows, b: dot(pair[0, rows, :], w[2, b].reshape(CG, CG), NT))
    shared(1).wait_recv()
    shared(2).wait_recv()
    scatter(
        1,
        lambda rows, b: dot(pair[1, rows, :], w[1, b].reshape(CG, CG), NT)
        + dot(pair[2, rows, :], w[0, b].reshape(CG, CG), NT),
    )
    collect(0, mixed_ref)
    collect(1, gin_ref)

    sent(snd, 0)
    sent(snd2, 1)
    for a in range(2):
        for b in range(NX):
            swap(a, b).wait_send()
    for i in every:
        give(i).wait_send()
        share(i).wait_send()
    for which in range(2):
        for b in range(NX):
            to_sibling(which, b).wait_send()
            home = jnp.logical_and(to_self, b == y_hi)

            @pl.when(jnp.logical_not(home))
            def _():
                onward(which, b).wait_send()

    for half in range(2):
        for i in every:
            for k in range(NK):
                out, device, _ = makers[half](i, k)
                copy(half, i, k, out, device).wait_send()


def body(features, grad_out, w_value, w_query, w_out, residues, decays, freqs, skips):
    first = lax.axis_index("ctx") * CB
    own = lambda a: lax.dynamic_slice_in_dim(a, first, CB, a.ndim - 1)
    flat = lambda a: own(a).T.reshape(1, LANES)
    skip_row = jnp.broadcast_to(own(skips)[:, None], (CB, ORDER)).reshape(1, LANES)
    prm = jnp.concatenate(
        [flat(decays), flat(freqs), flat(residues), skip_row, jnp.zeros((4, LANES), F32)], axis=0
    )
    vmem = pl.BlockSpec(memory_space=pltpu.VMEM)
    scratch = [
        pltpu.VMEM((3, NX, NZ, ROWS, CG), BF16),
        pltpu.VMEM((2, NX, 2 * TOK, CG), BF16),
        pltpu.VMEM((2 * TOK, CG), F32),
        pltpu.VMEM((3, TOK, CG), F32),
        pltpu.VMEM((3, TOK, CG), BF16),
        pltpu.VMEM((3, TOK, CG), BF16),
        pltpu.VMEM((TOK, CG), F32),
        pltpu.VMEM((TOK, CG), F32),
        pltpu.VMEM((NCTX, 2 * CB, TOK), BF16),
        pltpu.VMEM((NCTX, 2 * CB, TOK), BF16),
        pltpu.VMEM((NCTX, 2 * CB, TOK), BF16),
        pltpu.VMEM((NCTX, 2 * CB, TOK), BF16),
        pltpu.VMEM((NCTX * 2 * CB, TOK), F32),
        pltpu.VMEM((NCTX * 2 * CB, TOK), F32),
        pltpu.VMEM((CB * TOK, 2 * LANES), BF16),
        pltpu.VMEM((CB * TOK, 2 * LANES), BF16),
        pltpu.VMEM((2 * LANES, CB * TOK), BF16),
        pltpu.VMEM((2 * LANES, CB * TOK), BF16),
        pltpu.VMEM((CB, TOK, TOK), BF16),
        pltpu.VMEM((CB, TOK, TOK), BF16),
        pltpu.VMEM((LANES, TOK), F32),
        pltpu.VMEM((3, 2 * TOK, CG), BF16),
        pltpu.VMEM((2, NX, TOK, CG), BF16),
        pltpu.VMEM((2, NX, TOK, CG), BF16),
        pltpu.VMEM((2, NX, TOK, CG), BF16),
        pltpu.VMEM((2, NX, TOK, CG), BF16),
        pltpu.SemaphoreType.DMA((2, 3, NK)),
        pltpu.SemaphoreType.DMA((2, 3, NK)),
        pltpu.SemaphoreType.DMA((2, NX)),
        pltpu.SemaphoreType.DMA((2, 2, NX)),
        pltpu.SemaphoreType.DMA((2, 6)),
        pltpu.SemaphoreType.DMA((2, 2)),
        pltpu.SemaphoreType.DMA((2, 2, NX)),
        pltpu.SemaphoreType.DMA((2, 2, NX)),
    ]
    mixed, grad_in, res = pl.pallas_call(
        kernel,
        out_shape=(
            jax.ShapeDtypeStruct((TOK, CG), BF16),
            jax.ShapeDtypeStruct((TOK, CG), BF16),
            jax.ShapeDtypeStruct((8, LANES), F32),
        ),
        in_specs=[pl.BlockSpec(memory_space=pl.ANY)] * 2 + [vmem] * 4,
        out_specs=(vmem,) * 3,
        scratch_shapes=scratch,
        compiler_params=pltpu.CompilerParams(
            collective_id=0, has_side_effects=True, vmem_limit_bytes=48 * 2**20
        ),
        cost_estimate=pl.CostEstimate(
            flops=2 * 6 * TOK * CG * 4096, bytes_accessed=2**22, transcendentals=2**17
        ),
    )(features, grad_out, w_value, w_query, w_out.T, prm)
    return mixed, grad_in, res[0].reshape(CB, ORDER).T


def solution(mesh):
    placed = (
        P("ctx", None),
        P("ctx", None),
        P("ctx", "tp"),
        P("ctx", "tp"),
        P("tp", "ctx"),
        P(None, "tp"),
        P(None, "tp"),
        P(None, "tp"),
        P("tp"),
    )
    return jax.shard_map(
        body,
        mesh=mesh,
        in_specs=placed,
        out_specs=(P("ctx", "tp"), P("ctx", "tp"), P(None, ("tp", "ctx"))),
        check_vma=False,
    )
```

```python
import functools

import jax
import jax.numpy as jnp
from jax import lax
from jax.experimental import pallas as pl
from jax.experimental.pallas import tpu as pltpu
from jax.sharding import PartitionSpec as P

MESH = pl.DeviceIdType.MESH
F32, BF16 = jnp.float32, jnp.bfloat16
NX, NY, NZ = 4, 2, 8
NCTX, NTP = 64, 8
NXZ = NX * NZ
ROWS = 64
HALF = ROWS // 2
CG = 512
TOK = 128
CB = 8
ORDER = 16
LANES = CB * ORDER
NK = 20

NN = (((1,), (0,)), ((), ()))
NT = (((1,), (1,)), ((), ()))


def dot(a, b, dims=NN):
    return lax.dot_general(a, b, dims, preferred_element_type=F32)


def split(a):
    high = a.astype(BF16)
    return high, (a - high.astype(F32)).astype(BF16)


def build_tables(prm_ref, phi, plo, qhi, qlo, thi, tlo, bas):
    prm = prm_ref[...]
    row = lambda k: prm[k : k + 1, :]
    col = lambda k: jnp.broadcast_to(row(k), (LANES, LANES)).T
    d_row, f_row = row(0), row(1)
    d_col, f_col, r_col = col(0), col(1), col(2)
    lane = lax.broadcasted_iota(jnp.int32, (LANES, TOK), 1)
    sub = lax.broadcasted_iota(jnp.int32, (LANES, TOK), 0)
    t_q = (lane + 1).astype(F32)
    t_b = lane.astype(F32)
    t_p = (TOK - 1 - sub).astype(F32)
    mag = jnp.exp(-d_col * t_q)
    ang = f_col * t_q
    q_re, q_im = mag * jnp.cos(ang), mag * jnp.sin(ang)
    basis = jnp.exp(-d_col * t_b) * jnp.cos(f_col * t_b)
    bas[...] = basis
    mag = jnp.exp(-d_row * t_p)
    ang = f_row * t_p
    p_re, p_im = mag * jnp.cos(ang), mag * jnp.sin(ang)
    filt = jnp.sum((r_col * basis).reshape(CB, ORDER, TOK), axis=1)
    for c in range(CB):
        cols = slice(c * TOK, (c + 1) * TOK)
        own = lane // ORDER == c
        high, low = split(
            jnp.concatenate([jnp.where(own, p_re, 0.0), jnp.where(own, p_im, 0.0)], axis=1)
        )
        phi[cols, :] = high
        plo[cols, :] = low
        own = sub // ORDER == c
        high, low = split(
            jnp.concatenate([jnp.where(own, q_re, 0.0), jnp.where(own, q_im, 0.0)], axis=0)
        )
        qhi[:, cols] = high
        qlo[:, cols] = low
        rolled = pltpu.roll(
            jnp.broadcast_to(filt[c : c + 1, :], (TOK, TOK)), 0, 1, stride=1, stride_axis=0
        )
        skip = prm[3:4, c * ORDER : c * ORDER + 1]
        toep = jnp.where(lane >= sub, rolled, 0.0) + jnp.where(lane == sub, skip, 0.0)
        high, low = split(toep)
        thi[c] = high
        tlo[c] = low


def scan_chunks(re, im, lam, forward):
    at = lax.broadcasted_iota(jnp.int32, re.shape, 0)

    def shift(a, by):
        if forward:
            return jnp.where(at >= by, pltpu.roll(a, by, 0), 0.0)
        return jnp.where(at < NCTX - by, pltpu.roll(a, NCTX - by, 0), 0.0)

    re, im = shift(re, 1), shift(im, 1)
    by = 1
    for l_re, l_im in lam:
        s_re, s_im = shift(re, by), shift(im, by)
        re, im = re + l_re * s_re - l_im * s_im, im + l_re * s_im + l_im * s_re
        by *= 2
    return re, im


def chunk_step(prm_ref):
    prm = prm_ref[...]
    d_row, f_row = prm[0:1, :], prm[1:2, :]
    lam = []
    for k in range(6):
        span = float(TOK * 2**k)
        mag = jnp.exp(-d_row * span)
        lam.append((mag * jnp.cos(f_row * span), mag * jnp.sin(f_row * span)))
    return lam, prm[2:3, :]


def channels_of(ref):
    return [ref[pl.ds(c, NCTX, stride=CB), :].astype(BF16) for c in range(CB)]


def convolve(prm_ref, x32, y32, states, phi, plo, qhi, qlo, thi, tlo):
    lam, r_row = chunk_step(prm_ref)
    xs = channels_of(x32)
    xcat = jnp.concatenate(xs, axis=1)
    e = dot(xcat, phi[...]) + dot(xcat, plo[...])
    h_re, h_im = scan_chunks(e[:, :LANES], e[:, LANES:], lam, True)
    states[0] = h_re
    states[1] = h_im
    hh, hl = split(jnp.concatenate([r_row * h_re, -r_row * h_im], axis=1))
    y = dot(hh, qhi[...]) + dot(hl, qhi[...]) + dot(hh, qlo[...])
    for c in range(CB):
        cols = slice(c * TOK, (c + 1) * TOK)
        y32[pl.ds(c, NCTX, stride=CB), :] = y[:, cols] + dot(xs[c], thi[c]) + dot(xs[c], tlo[c])


def convolve_back(prm_ref, g32, z32, phi, plo, qhi, qlo, thi, tlo):
    lam, r_row = chunk_step(prm_ref)
    gs = channels_of(g32)
    gcat = jnp.concatenate(gs, axis=1)
    f = dot(gcat, qhi[...], NT) + dot(gcat, qlo[...], NT)
    k_re, k_im = scan_chunks(f[:, :LANES], f[:, LANES:], lam, False)
    kh, kl = split(jnp.concatenate([r_row * k_re, -r_row * k_im], axis=1))
    z = dot(kh, phi[...], NT) + dot(kl, phi[...], NT) + dot(kh, plo[...], NT)
    for c in range(CB):
        cols = slice(c * TOK, (c + 1) * TOK)
        z32[pl.ds(c, NCTX, stride=CB), :] = (
            z[:, cols] + dot(gs[c], thi[c], NT) + dot(gs[c], tlo[c], NT)
        )
    return gs, f


def amplitudes(x32, gs, f, states, bas, res_ref):
    across = jnp.sum(states[0] * f[:, :LANES] - states[1] * f[:, LANES:], axis=0, keepdims=True)
    lane = lax.broadcasted_iota(jnp.int32, (TOK, TOK), 1)
    sub = lax.broadcasted_iota(jnp.int32, (TOK, TOK), 0)
    flip = jnp.where(lane + sub == TOK - 1, 1.0, 0.0).astype(BF16)
    xs = channels_of(x32)
    corr = []
    for c in range(CB):
        back_t = dot(xs[c], flip).T.astype(BF16)
        pairs = dot(back_t, gs[c])
        lagged = pltpu.roll(pairs, 1, 1, stride=1, stride_axis=0)
        corr.append(jnp.sum(jnp.where(lane <= sub, lagged, 0.0), axis=0, keepdims=True))
    spread = jnp.concatenate([jnp.broadcast_to(a, (ORDER, TOK)) for a in corr], axis=0)
    within = jnp.sum((spread * bas[...]).T, axis=0, keepdims=True)
    res_ref[...] = jnp.broadcast_to(within + across, res_ref.shape)


def kernel(
    f_ref,
    g_ref,
    wv_ref,
    wq_ref,
    wo_ref,
    prm_ref,
    mixed_ref,
    gin_ref,
    res_ref,
    w,
    lhs,
    acc,
    turned,
    psnd,
    prcv,
    query,
    gg,
    state,
    snd,
    rcv,
    x32,
    g32,
    y32,
    states,
    phi,
    plo,
    qhi,
    qlo,
    thi,
    tlo,
    bas,
    pair,
    gat,
    part,
    sib,
    summed,
    got,
    ssem,
    rsem,
    lsem,
    fsem,
    ysem,
    xsem,
    csem,
    psem,
):
    ctx = lax.axis_index("ctx")
    tp = lax.axis_index("tp")
    xy = ctx // NZ
    x, y, z = xy // NY, xy % NY, ctx % NZ
    y_hi, core = tp // 2, tp % 2
    xl, xr, x2 = (x + NX - 1) % NX, (x + 1) % NX, (x + 2) % NX
    zl, zr = (z + NZ - 1) % NZ, (z + 1) % NZ
    yo = 1 - y
    at = lambda xi, yi, zi: (xi * NY + yi) * NZ + zi
    partner = (at(x, yo, z), tp)
    sibling = (ctx, y_hi * 2 + 1 - core)
    sum_ctx = at(x, core, z)
    to_self = core == y

    barrier = pltpu.get_barrier_semaphore()

    def greet(device):
        pl.semaphore_signal(barrier, inc=1, device_id=device, device_id_type=MESH)

    lane_of = x * NZ + z

    def mate(k):
        to = (lane_of + k) % NXZ
        return to, (at(to // NZ, y, to % NZ), tp)

    def greet_mate(k, carry):
        greet(mate(k)[1])
        return carry

    lax.fori_loop(1, NXZ, greet_mate, 0)
    greet(partner)
    greet(sibling)
    for k in range(1, NX):
        greet((sum_ctx, (y_hi + k) % NX * 2 + y))

    @pl.when(jnp.logical_not(to_self))
    def _():
        greet((sum_ctx, y_hi * 2 + y))

    def columns(block):
        return pl.ds(pl.multiple_of(block * CG, CG), CG)

    def token_rows(yi):
        return pl.ds(pl.multiple_of(yi * TOK, TOK), TOK)

    for i, ref in enumerate((wv_ref, wq_ref, wo_ref)):
        w[i, x, z] = ref[...]
    for a, ref in enumerate((f_ref, g_ref)):
        for b in range(NX):
            pltpu.make_async_copy(
                ref.at[:, columns(b * NY + y)], lhs.at[a, b, token_rows(y)], lsem.at[a, b]
            ).start()
    pl.semaphore_wait(barrier, NXZ - 1 + 2 + NX - 1 + jnp.where(to_self, 0, 1))

    def swap(a, b):
        return pltpu.make_async_remote_copy(
            src_ref=(f_ref, g_ref)[a].at[:, columns(b * NY + yo)],
            dst_ref=lhs.at[a, b, token_rows(y)],
            send_sem=fsem.at[0, a, b],
            recv_sem=fsem.at[1, a, b],
            device_id=partner,
            device_id_type=MESH,
        )

    for a in range(2):
        for b in range(NX):
            swap(a, b).start()

    def copy(half, i, k, ref, device):
        return pltpu.make_async_remote_copy(
            src_ref=ref,
            dst_ref=ref,
            send_sem=ssem.at[half, i, k],
            recv_sem=rsem.at[half, i, k],
            device_id=device,
            device_id_type=MESH,
        )

    to_r, to_l = (at(xr, y, z), tp), (at(xl, y, z), tp)
    to_u, to_d = (at(x, y, zr), tp), (at(x, y, zl), tp)
    quarter = HALF // 2
    first, second = pl.ds(0, HALF), pl.ds(HALF, HALF)

    def z_from(step, up):
        return (z + NZ - step) % NZ if up else (z + step) % NZ

    def a_copy(i, k):
        if k < 2:
            return w.at[i, x, z, first], (to_r, to_l)[k], w.at[i, (xl, xr)[k], z, first]
        if k < 4:
            rows = pl.ds((k - 2) * quarter, quarter)
            return w.at[i, (xl, xr)[k - 2], z, rows], (to_r, to_l)[k - 2], w.at[i, x2, z, rows]
        step, up, some = (k - 4) // 4, (k - 4) // 2 % 2 == 0, pl.ds(k % 2 * (NX // 2), NX // 2)
        return (
            w.at[i, some, z_from(step, up), first],
            to_u if up else to_d,
            w.at[i, some, z_from(step + 1, up), first],
        )

    def b_copy(i, k):
        if k < 8:
            up, step = k < 4, k % 4
            rows = second if step < 3 else pl.ds(HALF if up else HALF + quarter, quarter)
            return (
                w.at[i, x, z_from(step, up), rows],
                to_u if up else to_d,
                w.at[i, x, z_from(step + 1, up), rows],
            )
        if k < 12:
            way, some = (k - 8) // 2, pl.ds(k % 2 * (NZ // 2), NZ // 2)
            return (
                w.at[i, x, some, second],
                (to_r, to_l)[way],
                w.at[i, (xl, xr)[way], some, second],
            )
        way, some = k - 12, pl.ds((k - 12) * (NZ // 2), NZ // 2)
        return w.at[i, (xl, xr)[way], some, second], (to_r, to_l)[way], w.at[i, x2, some, second]

    used = (tuple(range(16)) + (16, 19), tuple(range(14)))
    makers = (a_copy, b_copy)

    def start(half, i, *ks):
        for k in ks:
            out, device, _ = makers[half](i, k)
            copy(half, i, k, out, device).start()

    def arrive(half, i, *ks):
        for k in ks:
            _, device, incoming = makers[half](i, k)
            copy(half, i, k, incoming, device).wait_recv()

    every = range(3)

    def a_start(i):
        arrive(0, i, 2, 3)
        start(0, i, 4, 6, 5, 7)

    def a_next(i, step):
        k = 4 + 4 * step
        for one in (k, k + 3, k + 1, k + 2):
            arrive(0, i, one)
            if one + 4 in used[0]:
                start(0, i, one + 4)

    def b_start(i):
        arrive(1, i, 3, 7)
        start(1, i, 8, 11, 9, 10)

    def b_second(i):
        arrive(1, i, 8)
        start(1, i, 12)
        arrive(1, i, 11)
        start(1, i, 13)

    def finish(i):
        arrive(0, i, 16, 19)
        arrive(1, i, 9, 10, 12, 13)

    def give(i):
        return pltpu.make_async_remote_copy(
            src_ref=psnd.at[i],
            dst_ref=prcv.at[i],
            send_sem=ysem.at[0, i],
            recv_sem=ysem.at[1, i],
            device_id=partner,
            device_id_type=MESH,
        )

    def project(a, i):
        acc[...] = jnp.zeros_like(acc)

        def step(b, carry):
            acc[...] += dot(lhs[a, b], w[i, b].reshape(CG, CG))
            return carry

        lax.fori_loop(0, NX, step, 0)
        turned[i] = acc[...].T.reshape(turned.shape[1:])
        psnd[i] = turned[i, :, yo].astype(BF16)
        give(i).start()

    def rows_in(a):
        for b in range(NX):
            pltpu.make_async_copy(
                (f_ref, g_ref)[a].at[:, columns(b * NY + y)],
                lhs.at[a, b, token_rows(y)],
                lsem.at[a, b],
            ).wait()
            swap(a, b).wait_recv()

    def total(i):
        give(i).wait_recv()
        return turned[i, :, y] + prcv[i].astype(F32)

    def exchange(which):
        def one(k, carry):
            to, device = mate(k)
            pltpu.make_async_remote_copy(
                src_ref=snd.at[which, to],
                dst_ref=rcv.at[which, lane_of],
                send_sem=xsem.at[which, 0],
                recv_sem=xsem.at[which, 1],
                device_id=device,
                device_id_type=MESH,
            ).start()
            return carry

        lax.fori_loop(1, NXZ, one, 0)
        rcv[which, lane_of] = snd[which, lane_of]

    def exchanged(which):
        rest = rcv.at[which, pl.ds(0, NXZ - 1)]
        pltpu.make_async_copy(rest, rest, xsem.at[which, 1]).wait()

    def to_chunks(which, a):
        a = a.reshape(NXZ, CB, 2 * TOK)
        snd[which] = jnp.concatenate([a[:, :, :TOK], a[:, :, TOK:]], axis=1).astype(BF16)

    def from_chunks(which):
        a = rcv[which].astype(F32)
        return jnp.concatenate([a[:, :CB], a[:, CB:]], axis=2).reshape(NX, ROWS, 2 * TOK)

    def chunks_in(which, ref):
        for xi in range(NX):
            a = rcv[which, xi * NZ : (xi + 1) * NZ].astype(F32)
            for yi in range(NY):
                at_row = (xi * NY + yi) * ROWS
                ref[at_row : at_row + ROWS, :] = a[:, yi * CB : (yi + 1) * CB].reshape(ROWS, TOK)

    def chunks_out(which):
        for xi in range(NX):
            both = [
                y32[(xi * NY + yi) * ROWS : (xi * NY + yi + 1) * ROWS, :].reshape(NZ, CB, TOK)
                for yi in range(NY)
            ]
            snd[which, xi * NZ : (xi + 1) * NZ] = jnp.concatenate(both, axis=1).astype(BF16)

    def share(i, yi):
        return pltpu.make_async_remote_copy(
            src_ref=pair.at[i, :, yi],
            dst_ref=pair.at[i, :, yi],
            send_sem=ysem.at[0, 3 + i],
            recv_sem=ysem.at[1, 3 + i],
            device_id=partner,
            device_id_type=MESH,
        )

    def put(i, a):
        pair[i, :, y] = a.astype(BF16)
        share(i, y).start()

    def shared(i):
        share(i, yo).wait_recv()
        gat[i] = pair[i].astype(F32).reshape(CG, 2 * TOK).T.astype(BF16)

    def to_sibling(which, b):
        return pltpu.make_async_remote_copy(
            src_ref=part.at[which, b],
            dst_ref=sib.at[which, b],
            send_sem=csem.at[0, which, b],
            recv_sem=csem.at[1, which, b],
            device_id=sibling,
            device_id_type=MESH,
        )

    def onward(which, b):
        return pltpu.make_async_remote_copy(
            src_ref=summed.at[which, b],
            dst_ref=got.at[which, y_hi],
            send_sem=psem.at[0, which, b],
            recv_sem=psem.at[1, which, y_hi],
            device_id=(sum_ctx, b * 2 + y),
            device_id_type=MESH,
        )

    def at_home(which):
        return pltpu.make_async_copy(
            summed.at[which, y_hi], got.at[which, y_hi], psem.at[1, which, y_hi]
        )

    def scatter(which, block):
        def give_half(k, carry):
            b = (y_hi + k) % NX
            part[which, b] = block(token_rows(1 - core), b).astype(BF16)
            to_sibling(which, b).start()
            return carry

        def send_on(k, carry):
            b = (y_hi + k) % NX
            mine = block(token_rows(core), b)
            to_sibling(which, b).wait_recv()
            summed[which, b] = (mine + sib[which, b].astype(F32)).astype(BF16)
            home = jnp.logical_and(to_self, b == y_hi)

            @pl.when(home)
            def _():
                at_home(which).start()

            @pl.when(jnp.logical_not(home))
            def _():
                onward(which, b).start()

            return carry

        lax.fori_loop(1, NX + 1, give_half, 0)
        lax.fori_loop(1, NX + 1, send_on, 0)

    def collect(which, out):
        total = None
        for k in range(NX):
            pltpu.make_async_copy(got.at[which, k], got.at[which, k], psem.at[1, which, k]).wait()
            term = got[which, k].astype(F32)
            total = term if k == 0 else total + term
        out[...] = total.astype(BF16)

    for i in every:
        start(0, i, 0, 1)
        start(1, i, 0, 4)
    for i in every:
        arrive(0, i, 0)
        start(0, i, 2)
        arrive(0, i, 1)
        start(0, i, 3)
        arrive(1, i, 0, 4)
        start(1, i, 1, 5)
    a_start(0)
    for i in every:
        arrive(1, i, 1, 5)
        start(1, i, 2, 6)
    for i in every:
        arrive(1, i, 2, 6)
        start(1, i, 3, 7)
    b_start(0)
    a_next(0, 0)
    a_start(1)
    a_next(0, 1)
    b_second(0)
    b_start(1)
    a_next(0, 2)
    a_next(1, 0)
    a_start(2)
    rows_in(0)
    finish(0)
    project(0, 0)
    a_next(1, 1)
    b_second(1)
    b_start(2)
    build_tables(prm_ref, phi, plo, qhi, qlo, thi, tlo, bas)
    to_chunks(0, total(0))
    exchange(0)
    a_next(2, 0)
    a_next(1, 2)
    exchanged(0)
    chunks_in(0, x32)
    convolve(prm_ref, x32, y32, states, phi, plo, qhi, qlo, thi, tlo)
    chunks_out(1)
    exchange(1)
    a_next(2, 1)
    b_second(2)
    finish(1)
    project(0, 1)
    a_next(2, 2)
    exchanged(1)
    state[...] = from_chunks(1)
    query[...] = total(1).astype(BF16).astype(F32)
    put(0, query[...] * state[...])
    rows_in(1)
    finish(2)
    project(1, 2)
    gg[...] = total(2)
    to_chunks(2, gg[...] * query[...])
    exchange(2)
    put(1, gg[...] * state[...])
    shared(0)
    scatter(0, lambda rows, b: dot(gat[0, rows, :], w[2, b].reshape(CG, CG), NT))
    exchanged(2)
    chunks_in(2, g32)
    gs, f = convolve_back(prm_ref, g32, y32, phi, plo, qhi, qlo, thi, tlo)
    chunks_out(3)
    exchange(3)
    amplitudes(x32, gs, f, states, bas, res_ref)
    shared(1)
    collect(0, mixed_ref)
    exchanged(3)
    put(2, from_chunks(3))
    shared(2)
    scatter(
        1,
        lambda rows, b: dot(gat[1, rows, :], w[1, b].reshape(CG, CG), NT)
        + dot(gat[2, rows, :], w[0, b].reshape(CG, CG), NT),
    )
    collect(1, gin_ref)

    for which in range(4):
        rest = snd.at[which, pl.ds(0, NXZ - 1)]
        pltpu.make_async_copy(rest, rest, xsem.at[which, 0]).wait()
    for a in range(2):
        for b in range(NX):
            swap(a, b).wait_send()
    for i in every:
        give(i).wait_send()
        share(i, y).wait_send()
    for which in range(2):
        for b in range(NX):
            to_sibling(which, b).wait_send()
            home = jnp.logical_and(to_self, b == y_hi)

            @pl.when(jnp.logical_not(home))
            def _():
                onward(which, b).wait_send()

    for half in range(2):
        for i in every:
            for k in used[half]:
                out, device, _ = makers[half](i, k)
                copy(half, i, k, out, device).wait_send()


def body(features, grad_out, w_value, w_query, w_out, residues, decays, freqs, skips):
    first = lax.axis_index("ctx") * CB
    own = lambda a: lax.dynamic_slice_in_dim(a, first, CB, a.ndim - 1)
    flat = lambda a: own(a).T.reshape(1, LANES)
    skip_row = jnp.broadcast_to(own(skips)[:, None], (CB, ORDER)).reshape(1, LANES)
    prm = jnp.concatenate(
        [flat(decays), flat(freqs), flat(residues), skip_row, jnp.zeros((4, LANES), F32)], axis=0
    )
    vmem = pl.BlockSpec(memory_space=pltpu.VMEM)
    scratch = [
        pltpu.VMEM((3, NX, NZ, ROWS, CG), BF16),
        pltpu.VMEM((2, NX, 2 * TOK, CG), BF16),
        pltpu.VMEM((2 * TOK, CG), F32),
        pltpu.VMEM((3, NX, NY, ROWS, 2 * TOK), F32),
        pltpu.VMEM((3, NX, ROWS, 2 * TOK), BF16),
        pltpu.VMEM((3, NX, ROWS, 2 * TOK), BF16),
        pltpu.VMEM((NX, ROWS, 2 * TOK), F32),
        pltpu.VMEM((NX, ROWS, 2 * TOK), F32),
        pltpu.VMEM((NX, ROWS, 2 * TOK), F32),
        pltpu.VMEM((4, NXZ, 2 * CB, TOK), BF16),
        pltpu.VMEM((4, NXZ, 2 * CB, TOK), BF16),
        pltpu.VMEM((NCTX * CB, TOK), F32),
        pltpu.VMEM((NCTX * CB, TOK), F32),
        pltpu.VMEM((NCTX * CB, TOK), F32),
        pltpu.VMEM((2, NCTX, LANES), F32),
        pltpu.VMEM((CB * TOK, 2 * LANES), BF16),
        pltpu.VMEM((CB * TOK, 2 * LANES), BF16),
        pltpu.VMEM((2 * LANES, CB * TOK), BF16),
        pltpu.VMEM((2 * LANES, CB * TOK), BF16),
        pltpu.VMEM((CB, TOK, TOK), BF16),
        pltpu.VMEM((CB, TOK, TOK), BF16),
        pltpu.VMEM((LANES, TOK), F32),
        pltpu.VMEM((3, NX, NY, ROWS, 2 * TOK), BF16),
        pltpu.VMEM((3, 2 * TOK, CG), BF16),
        pltpu.VMEM((2, NX, TOK, CG), BF16),
        pltpu.VMEM((2, NX, TOK, CG), BF16),
        pltpu.VMEM((2, NX, TOK, CG), BF16),
        pltpu.VMEM((2, NX, TOK, CG), BF16),
        pltpu.SemaphoreType.DMA((2, 3, NK)),
        pltpu.SemaphoreType.DMA((2, 3, NK)),
        pltpu.SemaphoreType.DMA((2, NX)),
        pltpu.SemaphoreType.DMA((2, 2, NX)),
        pltpu.SemaphoreType.DMA((2, 6)),
        pltpu.SemaphoreType.DMA((4, 2)),
        pltpu.SemaphoreType.DMA((2, 2, NX)),
        pltpu.SemaphoreType.DMA((2, 2, NX)),
    ]
    mixed, grad_in, res = pl.pallas_call(
        kernel,
        out_shape=(
            jax.ShapeDtypeStruct((TOK, CG), BF16),
            jax.ShapeDtypeStruct((TOK, CG), BF16),
            jax.ShapeDtypeStruct((8, LANES), F32),
        ),
        in_specs=[pl.BlockSpec(memory_space=pl.ANY)] * 2 + [vmem] * 4,
        out_specs=(vmem,) * 3,
        scratch_shapes=scratch,
        compiler_params=pltpu.CompilerParams(
            collective_id=0, has_side_effects=True, vmem_limit_bytes=48 * 2**20
        ),
        cost_estimate=pl.CostEstimate(
            flops=2 * 6 * TOK * CG * 4096, bytes_accessed=2**22, transcendentals=2**17
        ),
    )(features, grad_out, w_value, w_query, w_out.T, prm)
    return mixed, grad_in, res[0].reshape(CB, ORDER).T


def solution(mesh):
    placed = (
        P("ctx", None),
        P("ctx", None),
        P("ctx", "tp"),
        P("ctx", "tp"),
        P("tp", "ctx"),
        P(None, "tp"),
        P(None, "tp"),
        P(None, "tp"),
        P("tp"),
    )
    return jax.shard_map(
        body,
        mesh=mesh,
        in_specs=placed,
        out_specs=(P("ctx", "tp"), P("ctx", "tp"), P(None, ("tp", "ctx"))),
        check_vma=False,
    )
```

```python
import functools

import jax
import jax.numpy as jnp
from jax import lax
from jax.experimental import pallas as pl
from jax.experimental.pallas import tpu as pltpu
from jax.sharding import PartitionSpec as P

MESH = pl.DeviceIdType.MESH
F32, BF16 = jnp.float32, jnp.bfloat16
NX, NY, NZ = 4, 2, 8
NCTX, NTP = 64, 8
NXZ = NX * NZ
ROWS = 64
HALF = ROWS // 2
CG = 512
TOK = 128
CB = 8
ORDER = 16
LANES = CB * ORDER
NK = 20

NN = (((1,), (0,)), ((), ()))
NT = (((1,), (1,)), ((), ()))


def dot(a, b, dims=NN):
    return lax.dot_general(a, b, dims, preferred_element_type=F32)


def split(a):
    high = a.astype(BF16)
    return high, (a - high.astype(F32)).astype(BF16)


def build_tables(prm_ref, phi, plo, qhi, qlo, thi, tlo, bas):
    prm = prm_ref[...]
    row = lambda k: prm[k : k + 1, :]
    col = lambda k: jnp.broadcast_to(row(k), (LANES, LANES)).T
    d_row, f_row = row(0), row(1)
    d_col, f_col, r_col = col(0), col(1), col(2)
    lane = lax.broadcasted_iota(jnp.int32, (LANES, TOK), 1)
    sub = lax.broadcasted_iota(jnp.int32, (LANES, TOK), 0)
    t_q = (lane + 1).astype(F32)
    t_b = lane.astype(F32)
    t_p = (TOK - 1 - sub).astype(F32)
    mag = jnp.exp(-d_col * t_q)
    ang = f_col * t_q
    q_re, q_im = mag * jnp.cos(ang), mag * jnp.sin(ang)
    basis = jnp.exp(-d_col * t_b) * jnp.cos(f_col * t_b)
    bas[...] = basis
    mag = jnp.exp(-d_row * t_p)
    ang = f_row * t_p
    p_re, p_im = mag * jnp.cos(ang), mag * jnp.sin(ang)
    filt = jnp.sum((r_col * basis).reshape(CB, ORDER, TOK), axis=1)
    for c in range(CB):
        cols = slice(c * TOK, (c + 1) * TOK)
        own = lane // ORDER == c
        high, low = split(
            jnp.concatenate([jnp.where(own, p_re, 0.0), jnp.where(own, p_im, 0.0)], axis=1)
        )
        phi[cols, :] = high
        plo[cols, :] = low
        own = sub // ORDER == c
        high, low = split(
            jnp.concatenate([jnp.where(own, q_re, 0.0), jnp.where(own, q_im, 0.0)], axis=0)
        )
        qhi[:, cols] = high
        qlo[:, cols] = low
        rolled = pltpu.roll(
            jnp.broadcast_to(filt[c : c + 1, :], (TOK, TOK)), 0, 1, stride=1, stride_axis=0
        )
        skip = prm[3:4, c * ORDER : c * ORDER + 1]
        toep = jnp.where(lane >= sub, rolled, 0.0) + jnp.where(lane == sub, skip, 0.0)
        high, low = split(toep)
        thi[c] = high
        tlo[c] = low


def scan_chunks(re, im, lam, forward):
    at = lax.broadcasted_iota(jnp.int32, re.shape, 0)

    def shift(a, by):
        if forward:
            return jnp.where(at >= by, pltpu.roll(a, by, 0), 0.0)
        return jnp.where(at < NCTX - by, pltpu.roll(a, NCTX - by, 0), 0.0)

    re, im = shift(re, 1), shift(im, 1)
    by = 1
    for l_re, l_im in lam:
        s_re, s_im = shift(re, by), shift(im, by)
        re, im = re + l_re * s_re - l_im * s_im, im + l_re * s_im + l_im * s_re
        by *= 2
    return re, im


def pick_parameters(raw, skip, ctx, prm):
    every = jnp.concatenate([raw[...], jnp.broadcast_to(skip[...], (ORDER, CG))], axis=0)
    high, low = split(every)
    rest = (every - high.astype(F32) - low.astype(F32)).astype(BF16)
    channel = lax.broadcasted_iota(jnp.int32, (CG, LANES), 0)
    lane = lax.broadcasted_iota(jnp.int32, (CG, LANES), 1)
    one_hot = jnp.where(channel == ctx * CB + lane // ORDER, 1.0, 0.0).astype(BF16)
    spread = dot(high, one_hot) + dot(low, one_hot) + dot(rest, one_hot)
    mode = lax.broadcasted_iota(jnp.int32, (ORDER, LANES), 0)
    own = mode == lax.broadcasted_iota(jnp.int32, (ORDER, LANES), 1) % ORDER
    for k in range(4):
        rows = spread[k * ORDER : (k + 1) * ORDER, :]
        prm[k : k + 1, :] = jnp.sum(jnp.where(own, rows, 0.0), axis=0, keepdims=True)


def chunk_step(prm_ref):
    prm = prm_ref[...]
    d_row, f_row = prm[0:1, :], prm[1:2, :]
    lam = []
    for k in range(6):
        span = float(TOK * 2**k)
        mag = jnp.exp(-d_row * span)
        lam.append((mag * jnp.cos(f_row * span), mag * jnp.sin(f_row * span)))
    return lam, prm[2:3, :]


def channels_of(ref):
    return [ref[pl.ds(c, NCTX, stride=CB), :].astype(BF16) for c in range(CB)]


def convolve(prm_ref, x32, y32, states, phi, plo, qhi, qlo, thi, tlo):
    lam, r_row = chunk_step(prm_ref)
    xs = channels_of(x32)
    xcat = jnp.concatenate(xs, axis=1)
    e = dot(xcat, phi[...]) + dot(xcat, plo[...])
    h_re, h_im = scan_chunks(e[:, :LANES], e[:, LANES:], lam, True)
    states[0] = h_re
    states[1] = h_im
    hh, hl = split(jnp.concatenate([r_row * h_re, -r_row * h_im], axis=1))
    y = dot(hh, qhi[...]) + dot(hl, qhi[...]) + dot(hh, qlo[...])
    for c in range(CB):
        cols = slice(c * TOK, (c + 1) * TOK)
        y32[pl.ds(c, NCTX, stride=CB), :] = y[:, cols] + dot(xs[c], thi[c]) + dot(xs[c], tlo[c])


def convolve_back(prm_ref, g32, z32, phi, plo, qhi, qlo, thi, tlo):
    lam, r_row = chunk_step(prm_ref)
    gs = channels_of(g32)
    gcat = jnp.concatenate(gs, axis=1)
    f = dot(gcat, qhi[...], NT) + dot(gcat, qlo[...], NT)
    k_re, k_im = scan_chunks(f[:, :LANES], f[:, LANES:], lam, False)
    kh, kl = split(jnp.concatenate([r_row * k_re, -r_row * k_im], axis=1))
    z = dot(kh, phi[...], NT) + dot(kl, phi[...], NT) + dot(kh, plo[...], NT)
    for c in range(CB):
        cols = slice(c * TOK, (c + 1) * TOK)
        z32[pl.ds(c, NCTX, stride=CB), :] = (
            z[:, cols] + dot(gs[c], thi[c], NT) + dot(gs[c], tlo[c], NT)
        )
    return gs, f


def amplitudes(x32, gs, f, states, bas, res_ref):
    across = jnp.sum(states[0] * f[:, :LANES] - states[1] * f[:, LANES:], axis=0, keepdims=True)
    lane = lax.broadcasted_iota(jnp.int32, (TOK, TOK), 1)
    sub = lax.broadcasted_iota(jnp.int32, (TOK, TOK), 0)
    flip = jnp.where(lane + sub == TOK - 1, 1.0, 0.0).astype(BF16)
    xs = channels_of(x32)
    corr = []
    for c in range(CB):
        back_t = dot(xs[c], flip).T.astype(BF16)
        pairs = dot(back_t, gs[c])
        lagged = pltpu.roll(pairs, 1, 1, stride=1, stride_axis=0)
        corr.append(jnp.sum(jnp.where(lane <= sub, lagged, 0.0), axis=0, keepdims=True))
    spread = jnp.concatenate([jnp.broadcast_to(a, (ORDER, TOK)) for a in corr], axis=0)
    within = jnp.sum((spread * bas[...]).T, axis=0, keepdims=True)
    res_ref[...] = jnp.broadcast_to(within + across, res_ref.shape)


def kernel(
    f_ref,
    g_ref,
    wv_ref,
    wq_ref,
    wo_ref,
    decay_ref,
    freq_ref,
    amp_ref,
    skip_ref,
    mixed_ref,
    gin_ref,
    res_ref,
    raw,
    skip,
    prm_ref,
    w,
    lhs,
    acc,
    turned,
    psnd,
    prcv,
    query,
    gg,
    state,
    snd,
    rcv,
    x32,
    g32,
    y32,
    states,
    phi,
    plo,
    qhi,
    qlo,
    thi,
    tlo,
    bas,
    pair,
    gat,
    pre,
    part,
    sib,
    summed,
    got,
    ssem,
    rsem,
    gsem,
    lsem,
    fsem,
    ysem,
    xsem,
    csem,
    psem,
):
    ctx = lax.axis_index("ctx")
    tp = lax.axis_index("tp")
    xy = ctx // NZ
    x, y, z = xy // NY, xy % NY, ctx % NZ
    y_hi, core = tp // 2, tp % 2
    xl, xr, x2 = (x + NX - 1) % NX, (x + 1) % NX, (x + 2) % NX
    zl, zr = (z + NZ - 1) % NZ, (z + 1) % NZ
    yo = 1 - y
    at = lambda xi, yi, zi: (xi * NY + yi) * NZ + zi
    partner = (at(x, yo, z), tp)
    sibling = (ctx, y_hi * 2 + 1 - core)
    sum_ctx = at(x, core, z)
    to_self = core == y

    barrier = pltpu.get_barrier_semaphore()

    def greet(device):
        pl.semaphore_signal(barrier, inc=1, device_id=device, device_id_type=MESH)

    lane_of = x * NZ + z

    def mate(k):
        to = (lane_of + k) % NXZ
        return to, (at(to // NZ, y, to % NZ), tp)

    def greet_mate(k, carry):
        greet(mate(k)[1])
        return carry

    lax.fori_loop(1, NXZ, greet_mate, 0)
    greet(partner)
    greet(sibling)
    for k in range(1, NX):
        greet((sum_ctx, (y_hi + k) % NX * 2 + y))

    @pl.when(jnp.logical_not(to_self))
    def _():
        greet((sum_ctx, y_hi * 2 + y))

    def columns(block):
        return pl.ds(pl.multiple_of(block * CG, CG), CG)

    def token_rows(yi):
        return pl.ds(pl.multiple_of(yi * TOK, TOK), TOK)

    loads = [
        pltpu.make_async_copy(ref, w.at[i, x, z], gsem.at[i])
        for i, ref in enumerate((wv_ref, wq_ref, wo_ref))
    ]
    loads += [
        pltpu.make_async_copy(ref, raw.at[pl.ds(k * ORDER, ORDER)], gsem.at[3 + k])
        for k, ref in enumerate((decay_ref, freq_ref, amp_ref))
    ]
    loads.append(pltpu.make_async_copy(skip_ref, skip, gsem.at[6]))
    for one in loads:
        one.start()
    for a, ref in enumerate((f_ref, g_ref)):
        for b in range(NX):
            pltpu.make_async_copy(
                ref.at[:, columns(b * NY + y)], lhs.at[a, b, token_rows(y)], lsem.at[a, b]
            ).start()
    for one in loads:
        one.wait()
    pl.semaphore_wait(barrier, NXZ - 1 + 2 + NX - 1 + jnp.where(to_self, 0, 1))

    def swap(a, b):
        return pltpu.make_async_remote_copy(
            src_ref=(f_ref, g_ref)[a].at[:, columns(b * NY + yo)],
            dst_ref=lhs.at[a, b, token_rows(y)],
            send_sem=fsem.at[0, a, b],
            recv_sem=fsem.at[1, a, b],
            device_id=partner,
            device_id_type=MESH,
        )

    for a in range(2):
        for b in range(NX):
            swap(a, b).start()

    def copy(half, i, k, ref, device):
        return pltpu.make_async_remote_copy(
            src_ref=ref,
            dst_ref=ref,
            send_sem=ssem.at[half, i, k],
            recv_sem=rsem.at[half, i, k],
            device_id=device,
            device_id_type=MESH,
        )

    to_r, to_l = (at(xr, y, z), tp), (at(xl, y, z), tp)
    to_u, to_d = (at(x, y, zr), tp), (at(x, y, zl), tp)
    quarter = HALF // 2
    first, second = pl.ds(0, HALF), pl.ds(HALF, HALF)

    def z_from(step, up):
        return (z + NZ - step) % NZ if up else (z + step) % NZ

    def a_copy(i, k):
        if k < 2:
            return w.at[i, x, z, first], (to_r, to_l)[k], w.at[i, (xl, xr)[k], z, first]
        if k < 4:
            rows = pl.ds((k - 2) * quarter, quarter)
            return w.at[i, (xl, xr)[k - 2], z, rows], (to_r, to_l)[k - 2], w.at[i, x2, z, rows]
        step, up, some = (k - 4) // 4, (k - 4) // 2 % 2 == 0, pl.ds(k % 2 * (NX // 2), NX // 2)
        return (
            w.at[i, some, z_from(step, up), first],
            to_u if up else to_d,
            w.at[i, some, z_from(step + 1, up), first],
        )

    def b_copy(i, k):
        if k < 8:
            up, step = k < 4, k % 4
            rows = second if step < 3 else pl.ds(HALF if up else HALF + quarter, quarter)
            return (
                w.at[i, x, z_from(step, up), rows],
                to_u if up else to_d,
                w.at[i, x, z_from(step + 1, up), rows],
            )
        if k < 12:
            way, some = (k - 8) // 2, pl.ds(k % 2 * (NZ // 2), NZ // 2)
            return (
                w.at[i, x, some, second],
                (to_r, to_l)[way],
                w.at[i, (xl, xr)[way], some, second],
            )
        way, some = k - 12, pl.ds((k - 12) * (NZ // 2), NZ // 2)
        return w.at[i, (xl, xr)[way], some, second], (to_r, to_l)[way], w.at[i, x2, some, second]

    used = (tuple(range(16)) + (16, 19), tuple(range(14)))
    makers = (a_copy, b_copy)

    def start(half, i, *ks):
        for k in ks:
            out, device, _ = makers[half](i, k)
            copy(half, i, k, out, device).start()

    def arrive(half, i, *ks):
        for k in ks:
            _, device, incoming = makers[half](i, k)
            copy(half, i, k, incoming, device).wait_recv()

    every = range(3)

    def a_start(i):
        arrive(0, i, 2, 3)
        start(0, i, 4, 6, 5, 7)

    def a_next(i, step):
        k = 4 + 4 * step
        for one in (k, k + 3, k + 1, k + 2):
            arrive(0, i, one)
            if one + 4 in used[0]:
                start(0, i, one + 4)

    def b_start(i):
        arrive(1, i, 3, 7)
        start(1, i, 8, 11, 9, 10)

    def b_second(i):
        arrive(1, i, 8)
        start(1, i, 12)
        arrive(1, i, 11)
        start(1, i, 13)

    def finish(i):
        arrive(0, i, 16, 19)
        arrive(1, i, 9, 10, 12, 13)

    def give(i, part):
        some = pl.ds(part * (NX // 2), NX // 2)
        return pltpu.make_async_remote_copy(
            src_ref=psnd.at[i, some],
            dst_ref=prcv.at[i, some],
            send_sem=ysem.at[0, 2 * i + part],
            recv_sem=ysem.at[1, 2 * i + part],
            device_id=partner,
            device_id_type=MESH,
        )

    def project(a, i):
        wide = CG // 2
        for part in range(2):
            acc[...] = jnp.zeros_like(acc)

            def step(b, carry):
                cols = w[i, b, :, :, part * wide : (part + 1) * wide].reshape(CG, wide)
                acc[...] += dot(lhs[a, b], cols)
                return carry

            lax.fori_loop(0, NX, step, 0)
            some = slice(part * (NX // 2), (part + 1) * (NX // 2))
            turned[i, some] = acc[...].T.reshape(NX // 2, NY, ROWS, 2 * TOK)
            psnd[i, some] = turned[i, some, yo].astype(BF16)
            give(i, part).start()

    def rows_in(a):
        for b in range(NX):
            pltpu.make_async_copy(
                (f_ref, g_ref)[a].at[:, columns(b * NY + y)],
                lhs.at[a, b, token_rows(y)],
                lsem.at[a, b],
            ).wait()
            swap(a, b).wait_recv()

    def total(i):
        give(i, 0).wait_recv()
        give(i, 1).wait_recv()
        return turned[i, :, y] + prcv[i].astype(F32)

    def exchange(which):
        def one(k, carry):
            to, device = mate(k)
            pltpu.make_async_remote_copy(
                src_ref=snd.at[which, to],
                dst_ref=rcv.at[which, lane_of],
                send_sem=xsem.at[which, 0],
                recv_sem=xsem.at[which, 1],
                device_id=device,
                device_id_type=MESH,
            ).start()
            return carry

        lax.fori_loop(1, NXZ, one, 0)
        rcv[which, lane_of] = snd[which, lane_of]

    def exchanged(which):
        rest = rcv.at[which, pl.ds(0, NXZ - 1)]
        pltpu.make_async_copy(rest, rest, xsem.at[which, 1]).wait()

    def to_chunks(which, a):
        a = a.reshape(NXZ, CB, 2 * TOK)
        snd[which] = jnp.concatenate([a[:, :, :TOK], a[:, :, TOK:]], axis=1).astype(BF16)

    def from_chunks(which):
        a = rcv[which].astype(F32)
        return jnp.concatenate([a[:, :CB], a[:, CB:]], axis=2).reshape(NX, ROWS, 2 * TOK)

    def chunks_in(which, ref):
        for xi in range(NX):
            a = rcv[which, xi * NZ : (xi + 1) * NZ].astype(F32)
            for yi in range(NY):
                at_row = (xi * NY + yi) * ROWS
                ref[at_row : at_row + ROWS, :] = a[:, yi * CB : (yi + 1) * CB].reshape(ROWS, TOK)

    def chunks_out(which):
        for xi in range(NX):
            both = [
                y32[(xi * NY + yi) * ROWS : (xi * NY + yi + 1) * ROWS, :].reshape(NZ, CB, TOK)
                for yi in range(NY)
            ]
            snd[which, xi * NZ : (xi + 1) * NZ] = jnp.concatenate(both, axis=1).astype(BF16)

    def share(i, yi):
        return pltpu.make_async_remote_copy(
            src_ref=pair.at[i, :, yi],
            dst_ref=pair.at[i, :, yi],
            send_sem=ysem.at[0, 6 + i],
            recv_sem=ysem.at[1, 6 + i],
            device_id=partner,
            device_id_type=MESH,
        )

    def put(i, a):
        pair[i, :, y] = a.astype(BF16)
        share(i, y).start()

    def shared(i):
        share(i, yo).wait_recv()
        gat[i] = pair[i].astype(F32).reshape(CG, 2 * TOK).T.astype(BF16)

    def to_sibling(which, b):
        return pltpu.make_async_remote_copy(
            src_ref=part.at[which, b],
            dst_ref=sib.at[which, b],
            send_sem=csem.at[0, which, b],
            recv_sem=csem.at[1, which, b],
            device_id=sibling,
            device_id_type=MESH,
        )

    def onward(which, b):
        return pltpu.make_async_remote_copy(
            src_ref=summed.at[which, b],
            dst_ref=got.at[which, y_hi],
            send_sem=psem.at[0, which, b],
            recv_sem=psem.at[1, which, y_hi],
            device_id=(sum_ctx, b * 2 + y),
            device_id_type=MESH,
        )

    def at_home(which):
        return pltpu.make_async_copy(
            summed.at[which, y_hi], got.at[which, y_hi], psem.at[1, which, y_hi]
        )

    def scatter(which, block):
        def give_half(k):
            b = (y_hi + k) % NX
            part[which, b] = block(0, b).astype(BF16)
            to_sibling(which, b).start()

        def send_on(k):
            b = (y_hi + k) % NX
            mine = block(1, b)
            to_sibling(which, b).wait_recv()
            summed[which, b] = (mine + sib[which, b].astype(F32)).astype(BF16)
            if k == NX:
                home = jnp.logical_and(to_self, b == y_hi)

                @pl.when(home)
                def _():
                    at_home(which).start()

                @pl.when(jnp.logical_not(home))
                def _():
                    onward(which, b).start()
            else:
                onward(which, b).start()

        order = (2, 1, 3, 4)
        give_half(order[0])
        for k in range(NX):
            if k + 1 < NX:
                give_half(order[k + 1])
            send_on(order[k])

    halves = (token_rows(1 - core), token_rows(core))

    def early(b, carry):
        for k in range(2):
            pre[k, b] = dot(gat[1, halves[k], :], w[1, b].reshape(CG, CG), NT)
        return carry

    def collect(which, out):
        total = None
        for k in range(NX):
            pltpu.make_async_copy(got.at[which, k], got.at[which, k], psem.at[1, which, k]).wait()
            term = got[which, k].astype(F32)
            total = term if k == 0 else total + term
        out[...] = total.astype(BF16)

    for i in every:
        start(0, i, 0, 1)
        start(1, i, 0, 4)
    for i in every:
        arrive(0, i, 0)
        start(0, i, 2)
        arrive(0, i, 1)
        start(0, i, 3)
        arrive(1, i, 0, 4)
        start(1, i, 1, 5)
    a_start(0)
    for i in every:
        arrive(1, i, 1, 5)
        start(1, i, 2, 6)
    for i in every:
        arrive(1, i, 2, 6)
        start(1, i, 3, 7)
    b_start(0)
    a_next(0, 0)
    a_start(1)
    a_next(0, 1)
    b_second(0)
    b_start(1)
    a_next(0, 2)
    a_next(1, 0)
    a_start(2)
    rows_in(0)
    finish(0)
    project(0, 0)
    a_next(1, 1)
    b_second(1)
    b_start(2)
    pick_parameters(raw, skip, ctx, prm_ref)
    build_tables(prm_ref, phi, plo, qhi, qlo, thi, tlo, bas)
    to_chunks(0, total(0))
    exchange(0)
    a_next(2, 0)
    a_next(1, 2)
    exchanged(0)
    chunks_in(0, x32)
    convolve(prm_ref, x32, y32, states, phi, plo, qhi, qlo, thi, tlo)
    chunks_out(1)
    exchange(1)
    a_next(2, 1)
    b_second(2)
    finish(1)
    project(0, 1)
    a_next(2, 2)
    exchanged(1)
    state[...] = from_chunks(1)
    query[...] = total(1).astype(BF16).astype(F32)
    put(0, query[...] * state[...])
    rows_in(1)
    finish(2)
    project(1, 2)
    shared(0)
    gg[...] = total(2)
    to_chunks(2, gg[...] * query[...])
    exchange(2)
    put(1, gg[...] * state[...])
    scatter(0, lambda k, b: dot(gat[0, halves[k], :], w[2, b].reshape(CG, CG), NT))
    exchanged(2)
    chunks_in(2, g32)
    gs, f = convolve_back(prm_ref, g32, y32, phi, plo, qhi, qlo, thi, tlo)
    chunks_out(3)
    exchange(3)
    shared(1)
    lax.fori_loop(0, NX, early, 0)
    amplitudes(x32, gs, f, states, bas, res_ref)
    exchanged(3)
    put(2, from_chunks(3))
    shared(2)
    scatter(1, lambda k, b: pre[k, b] + dot(gat[2, halves[k], :], w[0, b].reshape(CG, CG), NT))
    collect(0, mixed_ref)
    collect(1, gin_ref)

    for which in range(4):
        rest = snd.at[which, pl.ds(0, NXZ - 1)]
        pltpu.make_async_copy(rest, rest, xsem.at[which, 0]).wait()
    for a in range(2):
        for b in range(NX):
            swap(a, b).wait_send()
    for i in every:
        give(i, 0).wait_send()
        give(i, 1).wait_send()
        share(i, y).wait_send()
    for which in range(2):
        for b in range(NX):
            to_sibling(which, b).wait_send()
            home = jnp.logical_and(to_self, b == y_hi)

            @pl.when(jnp.logical_not(home))
            def _():
                onward(which, b).wait_send()

    for half in range(2):
        for i in every:
            for k in used[half]:
                out, device, _ = makers[half](i, k)
                copy(half, i, k, out, device).wait_send()


def body(features, grad_out, w_value, w_query, w_out, residues, decays, freqs, skips):
    vmem = pl.BlockSpec(memory_space=pltpu.VMEM)
    scratch = [
        pltpu.VMEM((3 * ORDER, CG), F32),
        pltpu.VMEM((1, CG), F32),
        pltpu.VMEM((8, LANES), F32),
        pltpu.VMEM((3, NX, NZ, ROWS, CG), BF16),
        pltpu.VMEM((2, NX, 2 * TOK, CG), BF16),
        pltpu.VMEM((2 * TOK, CG // 2), F32),
        pltpu.VMEM((3, NX, NY, ROWS, 2 * TOK), F32),
        pltpu.VMEM((3, NX, ROWS, 2 * TOK), BF16),
        pltpu.VMEM((3, NX, ROWS, 2 * TOK), BF16),
        pltpu.VMEM((NX, ROWS, 2 * TOK), F32),
        pltpu.VMEM((NX, ROWS, 2 * TOK), F32),
        pltpu.VMEM((NX, ROWS, 2 * TOK), F32),
        pltpu.VMEM((4, NXZ, 2 * CB, TOK), BF16),
        pltpu.VMEM((4, NXZ, 2 * CB, TOK), BF16),
        pltpu.VMEM((NCTX * CB, TOK), F32),
        pltpu.VMEM((NCTX * CB, TOK), F32),
        pltpu.VMEM((NCTX * CB, TOK), F32),
        pltpu.VMEM((2, NCTX, LANES), F32),
        pltpu.VMEM((CB * TOK, 2 * LANES), BF16),
        pltpu.VMEM((CB * TOK, 2 * LANES), BF16),
        pltpu.VMEM((2 * LANES, CB * TOK), BF16),
        pltpu.VMEM((2 * LANES, CB * TOK), BF16),
        pltpu.VMEM((CB, TOK, TOK), BF16),
        pltpu.VMEM((CB, TOK, TOK), BF16),
        pltpu.VMEM((LANES, TOK), F32),
        pltpu.VMEM((3, NX, NY, ROWS, 2 * TOK), BF16),
        pltpu.VMEM((3, 2 * TOK, CG), BF16),
        pltpu.VMEM((2, NX, TOK, CG), F32),
        pltpu.VMEM((2, NX, TOK, CG), BF16),
        pltpu.VMEM((2, NX, TOK, CG), BF16),
        pltpu.VMEM((2, NX, TOK, CG), BF16),
        pltpu.VMEM((2, NX, TOK, CG), BF16),
        pltpu.SemaphoreType.DMA((2, 3, NK)),
        pltpu.SemaphoreType.DMA((2, 3, NK)),
        pltpu.SemaphoreType.DMA((7,)),
        pltpu.SemaphoreType.DMA((2, NX)),
        pltpu.SemaphoreType.DMA((2, 2, NX)),
        pltpu.SemaphoreType.DMA((2, 9)),
        pltpu.SemaphoreType.DMA((4, 2)),
        pltpu.SemaphoreType.DMA((2, 2, NX)),
        pltpu.SemaphoreType.DMA((2, 2, NX)),
    ]
    mixed, grad_in, res = pl.pallas_call(
        kernel,
        out_shape=(
            jax.ShapeDtypeStruct((TOK, CG), BF16),
            jax.ShapeDtypeStruct((TOK, CG), BF16),
            jax.ShapeDtypeStruct((8, LANES), F32),
        ),
        in_specs=[pl.BlockSpec(memory_space=pltpu.HBM)] * 9,
        out_specs=(vmem,) * 3,
        scratch_shapes=scratch,
        compiler_params=pltpu.CompilerParams(
            collective_id=0, has_side_effects=True, vmem_limit_bytes=63 * 2**20
        ),
        cost_estimate=pl.CostEstimate(
            flops=2 * 6 * TOK * CG * 4096, bytes_accessed=2**22, transcendentals=2**17
        ),
    )(features, grad_out, w_value, w_query, w_out.T, decays, freqs, residues, skips.reshape(1, CG))
    return mixed, grad_in, res[0].reshape(CB, ORDER).T


def solution(mesh):
    placed = (
        P("ctx", None),
        P("ctx", None),
        P("ctx", "tp"),
        P("ctx", "tp"),
        P("tp", "ctx"),
        P(None, "tp"),
        P(None, "tp"),
        P(None, "tp"),
        P("tp"),
    )
    return jax.shard_map(
        body,
        mesh=mesh,
        in_specs=placed,
        out_specs=(P("ctx", "tp"), P("ctx", "tp"), P(None, ("tp", "ctx"))),
        check_vma=False,
    )
```

```python
import functools

import jax
import jax.numpy as jnp
from jax import lax
from jax.experimental import pallas as pl
from jax.experimental.pallas import tpu as pltpu
from jax.sharding import PartitionSpec as P

MESH = pl.DeviceIdType.MESH
F32, BF16 = jnp.float32, jnp.bfloat16
NX, NY, NZ = 4, 2, 8
NCTX, NTP = 64, 8
NXZ = NX * NZ
ROWS = 64
HALF = ROWS // 2
CG = 512
TOK = 128
CB = 8
ORDER = 16
LANES = CB * ORDER
NK = 20

NN = (((1,), (0,)), ((), ()))
NT = (((1,), (1,)), ((), ()))


def dot(a, b, dims=NN):
    return lax.dot_general(a, b, dims, preferred_element_type=F32)


def split(a):
    high = a.astype(BF16)
    return high, (a - high.astype(F32)).astype(BF16)


def build_tables(prm_ref, phi, plo, qhi, qlo, thi, tlo, bas):
    prm = prm_ref[...]
    row = lambda k: prm[k : k + 1, :]
    col = lambda k: jnp.broadcast_to(row(k), (LANES, LANES)).T
    d_row, f_row = row(0), row(1)
    d_col, f_col, r_col = col(0), col(1), col(2)
    lane = lax.broadcasted_iota(jnp.int32, (LANES, TOK), 1)
    sub = lax.broadcasted_iota(jnp.int32, (LANES, TOK), 0)
    t_q = (lane + 1).astype(F32)
    t_b = lane.astype(F32)
    t_p = (TOK - 1 - sub).astype(F32)
    mag = jnp.exp(-d_col * t_q)
    ang = f_col * t_q
    q_re, q_im = mag * jnp.cos(ang), mag * jnp.sin(ang)
    basis = jnp.exp(-d_col * t_b) * jnp.cos(f_col * t_b)
    bas[...] = basis
    mag = jnp.exp(-d_row * t_p)
    ang = f_row * t_p
    p_re, p_im = mag * jnp.cos(ang), mag * jnp.sin(ang)
    filt = jnp.sum((r_col * basis).reshape(CB, ORDER, TOK), axis=1)
    for c in range(CB):
        cols = slice(c * TOK, (c + 1) * TOK)
        own = lane // ORDER == c
        high, low = split(
            jnp.concatenate([jnp.where(own, p_re, 0.0), jnp.where(own, p_im, 0.0)], axis=1)
        )
        phi[cols, :] = high
        plo[cols, :] = low
        own = sub // ORDER == c
        high, low = split(
            jnp.concatenate([jnp.where(own, q_re, 0.0), jnp.where(own, q_im, 0.0)], axis=0)
        )
        qhi[:, cols] = high
        qlo[:, cols] = low
        rolled = pltpu.roll(
            jnp.broadcast_to(filt[c : c + 1, :], (TOK, TOK)), 0, 1, stride=1, stride_axis=0
        )
        skip = prm[3:4, c * ORDER : c * ORDER + 1]
        toep = jnp.where(lane >= sub, rolled, 0.0) + jnp.where(lane == sub, skip, 0.0)
        high, low = split(toep)
        thi[c] = high
        tlo[c] = low


def scan_chunks(re, im, lam, forward):
    at = lax.broadcasted_iota(jnp.int32, re.shape, 0)

    def shift(a, by):
        if forward:
            return jnp.where(at >= by, pltpu.roll(a, by, 0), 0.0)
        return jnp.where(at < NCTX - by, pltpu.roll(a, NCTX - by, 0), 0.0)

    re, im = shift(re, 1), shift(im, 1)
    by = 1
    for l_re, l_im in lam:
        s_re, s_im = shift(re, by), shift(im, by)
        re, im = re + l_re * s_re - l_im * s_im, im + l_re * s_im + l_im * s_re
        by *= 2
    return re, im


def pick_parameters(raw, skip, ctx, prm):
    every = jnp.concatenate([raw[...], jnp.broadcast_to(skip[...], (ORDER, CG))], axis=0)
    high, low = split(every)
    rest = (every - high.astype(F32) - low.astype(F32)).astype(BF16)
    channel = lax.broadcasted_iota(jnp.int32, (CG, LANES), 0)
    lane = lax.broadcasted_iota(jnp.int32, (CG, LANES), 1)
    one_hot = jnp.where(channel == ctx * CB + lane // ORDER, 1.0, 0.0).astype(BF16)
    spread = dot(high, one_hot) + dot(low, one_hot) + dot(rest, one_hot)
    mode = lax.broadcasted_iota(jnp.int32, (ORDER, LANES), 0)
    own = mode == lax.broadcasted_iota(jnp.int32, (ORDER, LANES), 1) % ORDER
    for k in range(4):
        rows = spread[k * ORDER : (k + 1) * ORDER, :]
        prm[k : k + 1, :] = jnp.sum(jnp.where(own, rows, 0.0), axis=0, keepdims=True)


def chunk_step(prm_ref):
    prm = prm_ref[...]
    d_row, f_row = prm[0:1, :], prm[1:2, :]
    lam = []
    for k in range(6):
        span = float(TOK * 2**k)
        mag = jnp.exp(-d_row * span)
        lam.append((mag * jnp.cos(f_row * span), mag * jnp.sin(f_row * span)))
    return lam, prm[2:3, :]


def channels_of(ref):
    return [ref[pl.ds(c, NCTX, stride=CB), :].astype(BF16) for c in range(CB)]


def convolve(prm_ref, x32, y32, states, phi, plo, qhi, qlo, thi, tlo):
    lam, r_row = chunk_step(prm_ref)
    xs = channels_of(x32)
    xcat = jnp.concatenate(xs, axis=1)
    e = dot(xcat, phi[...]) + dot(xcat, plo[...])
    h_re, h_im = scan_chunks(e[:, :LANES], e[:, LANES:], lam, True)
    states[0] = h_re
    states[1] = h_im
    hh, hl = split(jnp.concatenate([r_row * h_re, -r_row * h_im], axis=1))
    y = dot(hh, qhi[...]) + dot(hl, qhi[...]) + dot(hh, qlo[...])
    for c in range(CB):
        cols = slice(c * TOK, (c + 1) * TOK)
        y32[pl.ds(c, NCTX, stride=CB), :] = y[:, cols] + dot(xs[c], thi[c]) + dot(xs[c], tlo[c])


def convolve_back(prm_ref, g32, z32, phi, plo, qhi, qlo, thi, tlo):
    lam, r_row = chunk_step(prm_ref)
    gs = channels_of(g32)
    gcat = jnp.concatenate(gs, axis=1)
    f = dot(gcat, qhi[...], NT) + dot(gcat, qlo[...], NT)
    k_re, k_im = scan_chunks(f[:, :LANES], f[:, LANES:], lam, False)
    kh, kl = split(jnp.concatenate([r_row * k_re, -r_row * k_im], axis=1))
    z = dot(kh, phi[...], NT) + dot(kl, phi[...], NT) + dot(kh, plo[...], NT)
    for c in range(CB):
        cols = slice(c * TOK, (c + 1) * TOK)
        z32[pl.ds(c, NCTX, stride=CB), :] = (
            z[:, cols] + dot(gs[c], thi[c], NT) + dot(gs[c], tlo[c], NT)
        )
    return gs, f


def amplitudes(x32, gs, f, states, bas, res_ref):
    across = jnp.sum(states[0] * f[:, :LANES] - states[1] * f[:, LANES:], axis=0, keepdims=True)
    lane = lax.broadcasted_iota(jnp.int32, (TOK, TOK), 1)
    sub = lax.broadcasted_iota(jnp.int32, (TOK, TOK), 0)
    flip = jnp.where(lane + sub == TOK - 1, 1.0, 0.0).astype(BF16)
    xs = channels_of(x32)
    corr = []
    for c in range(CB):
        back_t = dot(xs[c], flip).T.astype(BF16)
        pairs = dot(back_t, gs[c])
        lagged = pltpu.roll(pairs, 1, 1, stride=1, stride_axis=0)
        corr.append(jnp.sum(jnp.where(lane <= sub, lagged, 0.0), axis=0, keepdims=True))
    spread = jnp.concatenate([jnp.broadcast_to(a, (ORDER, TOK)) for a in corr], axis=0)
    within = jnp.sum((spread * bas[...]).T, axis=0, keepdims=True)
    res_ref[...] = jnp.broadcast_to(within + across, res_ref.shape)


def kernel(
    f_ref,
    g_ref,
    wv_ref,
    wq_ref,
    wo_ref,
    decay_ref,
    freq_ref,
    amp_ref,
    skip_ref,
    mixed_ref,
    gin_ref,
    res_ref,
    raw,
    skip,
    prm_ref,
    w,
    lhs,
    acc,
    turned,
    psnd,
    prcv,
    query,
    gg,
    state,
    snd,
    rcv,
    x32,
    g32,
    y32,
    states,
    phi,
    plo,
    qhi,
    qlo,
    thi,
    tlo,
    bas,
    pair,
    gat,
    pre,
    part,
    sib,
    summed,
    got,
    ssem,
    rsem,
    gsem,
    lsem,
    fsem,
    ysem,
    xsem,
    csem,
    psem,
):
    ctx = lax.axis_index("ctx")
    tp = lax.axis_index("tp")
    xy = ctx // NZ
    x, y, z = xy // NY, xy % NY, ctx % NZ
    y_hi, core = tp // 2, tp % 2
    xl, xr, x2 = (x + NX - 1) % NX, (x + 1) % NX, (x + 2) % NX
    zl, zr = (z + NZ - 1) % NZ, (z + 1) % NZ
    yo = 1 - y
    at = lambda xi, yi, zi: (xi * NY + yi) * NZ + zi
    partner = (at(x, yo, z), tp)
    sibling = (ctx, y_hi * 2 + 1 - core)
    sum_ctx = at(x, core, z)
    to_self = core == y

    barrier = pltpu.get_barrier_semaphore()

    def greet(device):
        pl.semaphore_signal(barrier, inc=1, device_id=device, device_id_type=MESH)

    lane_of = x * NZ + z

    def mate(k):
        to = (lane_of + k) % NXZ
        return to, (at(to // NZ, y, to % NZ), tp)

    def greet_mate(k, carry):
        greet(mate(k)[1])
        return carry

    lax.fori_loop(1, NXZ, greet_mate, 0)
    greet(partner)
    greet(sibling)
    for k in range(1, NX):
        greet((sum_ctx, (y_hi + k) % NX * 2 + y))

    @pl.when(jnp.logical_not(to_self))
    def _():
        greet((sum_ctx, y_hi * 2 + y))

    def columns(block):
        return pl.ds(pl.multiple_of(block * CG, CG), CG)

    def token_rows(yi):
        return pl.ds(pl.multiple_of(yi * TOK, TOK), TOK)

    loads = [
        pltpu.make_async_copy(ref, w.at[i, x, z], gsem.at[i])
        for i, ref in enumerate((wv_ref, wq_ref, wo_ref))
    ]
    loads += [
        pltpu.make_async_copy(ref, raw.at[pl.ds(k * ORDER, ORDER)], gsem.at[3 + k])
        for k, ref in enumerate((decay_ref, freq_ref, amp_ref))
    ]
    loads.append(pltpu.make_async_copy(skip_ref, skip, gsem.at[6]))
    for one in loads:
        one.start()
    for a, ref in enumerate((f_ref, g_ref)):
        for b in range(NX):
            pltpu.make_async_copy(
                ref.at[:, columns(b * NY + y)], lhs.at[a, b, token_rows(y)], lsem.at[a, b]
            ).start()
    for one in loads:
        one.wait()
    pl.semaphore_wait(barrier, NXZ - 1 + 2 + NX - 1 + jnp.where(to_self, 0, 1))

    def swap(a, b):
        return pltpu.make_async_remote_copy(
            src_ref=(f_ref, g_ref)[a].at[:, columns(b * NY + yo)],
            dst_ref=lhs.at[a, b, token_rows(y)],
            send_sem=fsem.at[0, a, b],
            recv_sem=fsem.at[1, a, b],
            device_id=partner,
            device_id_type=MESH,
        )

    for a in range(2):
        for b in range(NX):
            swap(a, b).start()

    def copy(half, i, k, ref, device):
        return pltpu.make_async_remote_copy(
            src_ref=ref,
            dst_ref=ref,
            send_sem=ssem.at[half, i, k],
            recv_sem=rsem.at[half, i, k],
            device_id=device,
            device_id_type=MESH,
        )

    to_r, to_l = (at(xr, y, z), tp), (at(xl, y, z), tp)
    to_u, to_d = (at(x, y, zr), tp), (at(x, y, zl), tp)
    quarter = HALF // 2
    first, second = pl.ds(0, HALF), pl.ds(HALF, HALF)

    def z_from(step, up):
        return (z + NZ - step) % NZ if up else (z + step) % NZ

    def a_copy(i, k):
        if k < 2:
            return w.at[i, x, z, first], (to_r, to_l)[k], w.at[i, (xl, xr)[k], z, first]
        if k < 4:
            rows = pl.ds((k - 2) * quarter, quarter)
            return w.at[i, (xl, xr)[k - 2], z, rows], (to_r, to_l)[k - 2], w.at[i, x2, z, rows]
        step, up, some = (k - 4) // 4, (k - 4) // 2 % 2 == 0, pl.ds(k % 2 * (NX // 2), NX // 2)
        return (
            w.at[i, some, z_from(step, up), first],
            to_u if up else to_d,
            w.at[i, some, z_from(step + 1, up), first],
        )

    def b_copy(i, k):
        if k < 8:
            up, step = k < 4, k % 4
            rows = second if step < 3 else pl.ds(HALF if up else HALF + quarter, quarter)
            return (
                w.at[i, x, z_from(step, up), rows],
                to_u if up else to_d,
                w.at[i, x, z_from(step + 1, up), rows],
            )
        if k < 12:
            way, some = (k - 8) // 2, pl.ds(k % 2 * (NZ // 2), NZ // 2)
            return (
                w.at[i, x, some, second],
                (to_r, to_l)[way],
                w.at[i, (xl, xr)[way], some, second],
            )
        way, some = k - 12, pl.ds((k - 12) * (NZ // 2), NZ // 2)
        return w.at[i, (xl, xr)[way], some, second], (to_r, to_l)[way], w.at[i, x2, some, second]

    used = (tuple(range(16)) + (16, 19), tuple(range(14)))
    makers = (a_copy, b_copy)

    def start(half, i, *ks):
        for k in ks:
            out, device, _ = makers[half](i, k)
            copy(half, i, k, out, device).start()

    def arrive(half, i, *ks):
        for k in ks:
            _, device, incoming = makers[half](i, k)
            copy(half, i, k, incoming, device).wait_recv()

    every = range(3)

    def a_start(i):
        arrive(0, i, 2, 3)
        start(0, i, 4, 6, 5, 7)

    def a_next(i, step):
        k = 4 + 4 * step
        for one in (k, k + 3, k + 1, k + 2):
            arrive(0, i, one)
            if one + 4 in used[0]:
                start(0, i, one + 4)

    def b_start(i):
        arrive(1, i, 3, 7)
        start(1, i, 8, 11, 9, 10)

    def b_second(i):
        arrive(1, i, 8)
        start(1, i, 12)
        arrive(1, i, 11)
        start(1, i, 13)

    def finish(i):
        arrive(0, i, 16, 19)
        arrive(1, i, 9, 10, 12, 13)

    def give(i, part):
        some = pl.ds(part * (NX // 2), NX // 2)
        return pltpu.make_async_remote_copy(
            src_ref=psnd.at[i, some],
            dst_ref=prcv.at[i, some],
            send_sem=ysem.at[0, 2 * i + part],
            recv_sem=ysem.at[1, 2 * i + part],
            device_id=partner,
            device_id_type=MESH,
        )

    def project(a, i):
        wide = CG // 2
        for part in range(2):
            acc[...] = jnp.zeros_like(acc)

            def step(b, carry):
                cols = w[i, b, :, :, part * wide : (part + 1) * wide].reshape(CG, wide)
                acc[...] += dot(lhs[a, b], cols)
                return carry

            lax.fori_loop(0, NX, step, 0)
            some = slice(part * (NX // 2), (part + 1) * (NX // 2))
            turned[i, some] = acc[...].T.reshape(NX // 2, NY, ROWS, 2 * TOK)
            psnd[i, some] = turned[i, some, yo].astype(BF16)
            give(i, part).start()

    def rows_in(a):
        for b in range(NX):
            pltpu.make_async_copy(
                (f_ref, g_ref)[a].at[:, columns(b * NY + y)],
                lhs.at[a, b, token_rows(y)],
                lsem.at[a, b],
            ).wait()
            swap(a, b).wait_recv()

    def total(i):
        give(i, 0).wait_recv()
        give(i, 1).wait_recv()
        return turned[i, :, y] + prcv[i].astype(F32)

    def exchange(which):
        def one(k, carry):
            to, device = mate(k)
            pltpu.make_async_remote_copy(
                src_ref=snd.at[which, to],
                dst_ref=rcv.at[which, lane_of],
                send_sem=xsem.at[which, 0],
                recv_sem=xsem.at[which, 1],
                device_id=device,
                device_id_type=MESH,
            ).start()
            return carry

        lax.fori_loop(1, NXZ, one, 0)
        rcv[which, lane_of] = snd[which, lane_of]

    def exchanged(which):
        rest = rcv.at[which, pl.ds(0, NXZ - 1)]
        pltpu.make_async_copy(rest, rest, xsem.at[which, 1]).wait()

    def to_chunks(which, a):
        a = a.reshape(NXZ, CB, 2 * TOK)
        snd[which] = jnp.concatenate([a[:, :, :TOK], a[:, :, TOK:]], axis=1).astype(BF16)

    def from_chunks(which):
        a = rcv[which].astype(F32)
        return jnp.concatenate([a[:, :CB], a[:, CB:]], axis=2).reshape(NX, ROWS, 2 * TOK)

    def chunks_in(which, ref):
        for xi in range(NX):
            a = rcv[which, xi * NZ : (xi + 1) * NZ].astype(F32)
            for yi in range(NY):
                at_row = (xi * NY + yi) * ROWS
                ref[at_row : at_row + ROWS, :] = a[:, yi * CB : (yi + 1) * CB].reshape(ROWS, TOK)

    def chunks_out(which):
        for xi in range(NX):
            both = [
                y32[(xi * NY + yi) * ROWS : (xi * NY + yi + 1) * ROWS, :].reshape(NZ, CB, TOK)
                for yi in range(NY)
            ]
            snd[which, xi * NZ : (xi + 1) * NZ] = jnp.concatenate(both, axis=1).astype(BF16)

    def share(i, yi):
        return pltpu.make_async_remote_copy(
            src_ref=pair.at[i, :, yi],
            dst_ref=pair.at[i, :, yi],
            send_sem=ysem.at[0, 6 + i],
            recv_sem=ysem.at[1, 6 + i],
            device_id=partner,
            device_id_type=MESH,
        )

    def put(i, a):
        pair[i, :, y] = a.astype(BF16)
        share(i, y).start()

    def shared(i):
        share(i, yo).wait_recv()
        gat[i] = pair[i].astype(F32).reshape(CG, 2 * TOK).T.astype(BF16)

    def to_sibling(which, b):
        return pltpu.make_async_remote_copy(
            src_ref=part.at[which, b],
            dst_ref=sib.at[which, b],
            send_sem=csem.at[0, which, b],
            recv_sem=csem.at[1, which, b],
            device_id=sibling,
            device_id_type=MESH,
        )

    def onward(which, b):
        return pltpu.make_async_remote_copy(
            src_ref=summed.at[which, b],
            dst_ref=got.at[which, y_hi],
            send_sem=psem.at[0, which, b],
            recv_sem=psem.at[1, which, y_hi],
            device_id=(sum_ctx, b * 2 + y),
            device_id_type=MESH,
        )

    def at_home(which):
        return pltpu.make_async_copy(
            summed.at[which, y_hi], got.at[which, y_hi], psem.at[1, which, y_hi]
        )

    def scatter(which, block):
        def give_half(k):
            b = (y_hi + k) % NX
            part[which, b] = block(0, b).astype(BF16)
            to_sibling(which, b).start()

        def send_on(k):
            b = (y_hi + k) % NX
            mine = block(1, b)
            to_sibling(which, b).wait_recv()
            summed[which, b] = (mine + sib[which, b].astype(F32)).astype(BF16)
            if k == NX:
                home = jnp.logical_and(to_self, b == y_hi)

                @pl.when(home)
                def _():
                    at_home(which).start()

                @pl.when(jnp.logical_not(home))
                def _():
                    onward(which, b).start()
            else:
                onward(which, b).start()

        order = (2, 1, 3, 4)
        give_half(order[0])
        for k in range(NX):
            if k + 1 < NX:
                give_half(order[k + 1])
            send_on(order[k])

    halves = (token_rows(1 - core), token_rows(core))

    def early(b, carry):
        for k in range(2):
            pre[k, b] = dot(gat[1, halves[k], :], w[1, b].reshape(CG, CG), NT)
        return carry

    def collect(which, out):
        total = None
        for k in range(NX):
            pltpu.make_async_copy(got.at[which, k], got.at[which, k], psem.at[1, which, k]).wait()
            term = got[which, k].astype(F32)
            total = term if k == 0 else total + term
        out[...] = total.astype(BF16)

    for i in every:
        start(0, i, 0, 1)
        start(1, i, 0, 4)
    for i in every:
        arrive(0, i, 0)
        start(0, i, 2)
        arrive(0, i, 1)
        start(0, i, 3)
        arrive(1, i, 0, 4)
        start(1, i, 1, 5)
    a_start(0)
    for i in every:
        arrive(1, i, 1, 5)
        start(1, i, 2, 6)
    for i in every:
        arrive(1, i, 2, 6)
        start(1, i, 3, 7)
    b_start(0)
    a_next(0, 0)
    a_start(1)
    a_next(0, 1)
    b_second(0)
    b_start(1)
    a_next(0, 2)
    a_next(1, 0)
    a_start(2)
    rows_in(0)
    finish(0)
    project(0, 0)
    a_next(1, 1)
    b_second(1)
    b_start(2)
    pick_parameters(raw, skip, ctx, prm_ref)
    build_tables(prm_ref, phi, plo, qhi, qlo, thi, tlo, bas)
    to_chunks(0, total(0))
    exchange(0)
    a_next(2, 0)
    a_next(1, 2)
    exchanged(0)
    chunks_in(0, x32)
    convolve(prm_ref, x32, y32, states, phi, plo, qhi, qlo, thi, tlo)
    chunks_out(1)
    exchange(1)
    a_next(2, 1)
    b_second(2)
    finish(1)
    project(0, 1)
    a_next(2, 2)
    exchanged(1)
    state[...] = from_chunks(1)
    query[...] = total(1).astype(BF16).astype(F32)
    put(0, query[...] * state[...])
    rows_in(1)
    finish(2)
    project(1, 2)
    shared(0)
    gg[...] = total(2)
    to_chunks(2, gg[...] * query[...])
    exchange(2)
    put(1, gg[...] * state[...])
    scatter(0, lambda k, b: dot(gat[0, halves[k], :], w[2, b].reshape(CG, CG), NT))
    exchanged(2)
    chunks_in(2, g32)
    gs, f = convolve_back(prm_ref, g32, y32, phi, plo, qhi, qlo, thi, tlo)
    chunks_out(3)
    exchange(3)
    shared(1)
    lax.fori_loop(0, NX, early, 0)
    exchanged(3)
    put(2, from_chunks(3))
    shared(2)
    scatter(1, lambda k, b: pre[k, b] + dot(gat[2, halves[k], :], w[0, b].reshape(CG, CG), NT))
    amplitudes(x32, gs, f, states, bas, res_ref)
    collect(0, mixed_ref)
    collect(1, gin_ref)

    for which in range(4):
        rest = snd.at[which, pl.ds(0, NXZ - 1)]
        pltpu.make_async_copy(rest, rest, xsem.at[which, 0]).wait()
    for a in range(2):
        for b in range(NX):
            swap(a, b).wait_send()
    for i in every:
        give(i, 0).wait_send()
        give(i, 1).wait_send()
        share(i, y).wait_send()
    for which in range(2):
        for b in range(NX):
            to_sibling(which, b).wait_send()
            home = jnp.logical_and(to_self, b == y_hi)

            @pl.when(jnp.logical_not(home))
            def _():
                onward(which, b).wait_send()

    for half in range(2):
        for i in every:
            for k in used[half]:
                out, device, _ = makers[half](i, k)
                copy(half, i, k, out, device).wait_send()


def body(features, grad_out, w_value, w_query, w_out, residues, decays, freqs, skips):
    vmem = pl.BlockSpec(memory_space=pltpu.VMEM)
    scratch = [
        pltpu.VMEM((3 * ORDER, CG), F32),
        pltpu.VMEM((1, CG), F32),
        pltpu.VMEM((8, LANES), F32),
        pltpu.VMEM((3, NX, NZ, ROWS, CG), BF16),
        pltpu.VMEM((2, NX, 2 * TOK, CG), BF16),
        pltpu.VMEM((2 * TOK, CG // 2), F32),
        pltpu.VMEM((3, NX, NY, ROWS, 2 * TOK), F32),
        pltpu.VMEM((3, NX, ROWS, 2 * TOK), BF16),
        pltpu.VMEM((3, NX, ROWS, 2 * TOK), BF16),
        pltpu.VMEM((NX, ROWS, 2 * TOK), F32),
        pltpu.VMEM((NX, ROWS, 2 * TOK), F32),
        pltpu.VMEM((NX, ROWS, 2 * TOK), F32),
        pltpu.VMEM((4, NXZ, 2 * CB, TOK), BF16),
        pltpu.VMEM((4, NXZ, 2 * CB, TOK), BF16),
        pltpu.VMEM((NCTX * CB, TOK), F32),
        pltpu.VMEM((NCTX * CB, TOK), F32),
        pltpu.VMEM((NCTX * CB, TOK), F32),
        pltpu.VMEM((2, NCTX, LANES), F32),
        pltpu.VMEM((CB * TOK, 2 * LANES), BF16),
        pltpu.VMEM((CB * TOK, 2 * LANES), BF16),
        pltpu.VMEM((2 * LANES, CB * TOK), BF16),
        pltpu.VMEM((2 * LANES, CB * TOK), BF16),
        pltpu.VMEM((CB, TOK, TOK), BF16),
        pltpu.VMEM((CB, TOK, TOK), BF16),
        pltpu.VMEM((LANES, TOK), F32),
        pltpu.VMEM((3, NX, NY, ROWS, 2 * TOK), BF16),
        pltpu.VMEM((3, 2 * TOK, CG), BF16),
        pltpu.VMEM((2, NX, TOK, CG), F32),
        pltpu.VMEM((2, NX, TOK, CG), BF16),
        pltpu.VMEM((2, NX, TOK, CG), BF16),
        pltpu.VMEM((2, NX, TOK, CG), BF16),
        pltpu.VMEM((2, NX, TOK, CG), BF16),
        pltpu.SemaphoreType.DMA((2, 3, NK)),
        pltpu.SemaphoreType.DMA((2, 3, NK)),
        pltpu.SemaphoreType.DMA((7,)),
        pltpu.SemaphoreType.DMA((2, NX)),
        pltpu.SemaphoreType.DMA((2, 2, NX)),
        pltpu.SemaphoreType.DMA((2, 9)),
        pltpu.SemaphoreType.DMA((4, 2)),
        pltpu.SemaphoreType.DMA((2, 2, NX)),
        pltpu.SemaphoreType.DMA((2, 2, NX)),
    ]
    mixed, grad_in, res = pl.pallas_call(
        kernel,
        out_shape=(
            jax.ShapeDtypeStruct((TOK, CG), BF16),
            jax.ShapeDtypeStruct((TOK, CG), BF16),
            jax.ShapeDtypeStruct((8, LANES), F32),
        ),
        in_specs=[pl.BlockSpec(memory_space=pltpu.HBM)] * 9,
        out_specs=(vmem,) * 3,
        scratch_shapes=scratch,
        compiler_params=pltpu.CompilerParams(
            collective_id=0, has_side_effects=True, vmem_limit_bytes=63 * 2**20
        ),
        cost_estimate=pl.CostEstimate(
            flops=2 * 6 * TOK * CG * 4096, bytes_accessed=2**22, transcendentals=2**17
        ),
    )(features, grad_out, w_value, w_query, w_out.T, decays, freqs, residues, skips.reshape(1, CG))
    return mixed, grad_in, res[0].reshape(CB, ORDER).T


def solution(mesh):
    placed = (
        P("ctx", None),
        P("ctx", None),
        P("ctx", "tp"),
        P("ctx", "tp"),
        P("tp", "ctx"),
        P(None, "tp"),
        P(None, "tp"),
        P(None, "tp"),
        P("tp"),
    )
    return jax.shard_map(
        body,
        mesh=mesh,
        in_specs=placed,
        out_specs=(P("ctx", "tp"), P("ctx", "tp"), P(None, ("tp", "ctx"))),
        check_vma=False,
    )
```
